512 devices in a mesh: gx: 32 (over z_hi, x, core), gy: 16 (over y, z_lo).
Axes of the slice: x: 4, y: 4, z: 16 (z_hi: 4, z_lo: 4; z = z_hi * 4 + z_lo), core: 2. Of those that a mesh axis runs over, the one named last changes fastest.
Arguments:
- feats: bfloat16 [32, 16, 2, 128, 512], P('gx', 'gy'), may hold values from -12 to 12
- w_query: bfloat16 [512, 512], replicated, may hold values from -1 to 1
- w_key: bfloat16 [512, 512], replicated, may hold values from -1 to 1
- w_value: bfloat16 [512, 512], replicated, may hold values from -0.25 to 0.25
- out_grad: bfloat16 [32, 16, 2, 128, 512], P('gx', 'gy'), may hold values from -6 to 6
- patch_count: int32 [32, 16], P('gx', 'gy'), may hold values from 1 to 2
- point_count: int32 [32, 16, 2], P('gx', 'gy'), may hold values from 32 to 128
- neighbours: int32 [32, 16, 2, 3], P('gx', 'gy'), may hold values from 0 to 9, as said below
- neighbour_points: int32 [32, 16, 2, 3], P('gx', 'gy'), may hold values from 32 to 128, as said below
Outputs:
- mixed: bfloat16 [32, 16, 2, 128, 512], P('gx', 'gy')
- feat_grad: bfloat16 [32, 16, 2, 128, 512], P('gx', 'gy')
- grad_query: bfloat16 [512, 512], replicated
- grad_key: bfloat16 [512, 512], replicated
- grad_value: bfloat16 [512, 512], replicated
The draws below stay inside these ranges and needn't reach their ends.
Inputs may be any that keep to these rules, and one draw needn't show every extreme that they name: `neighbours`: A code c names slot c % 2 of the device c // 2 steps away as in the reference program; that device lies inside the grid and that slot is below its patch_count. `neighbour_points`: equal to point_count of the patch that the same entry of neighbours names.
All inputs are finite; a program needn't handle non-finite values.
Results may differ from the reference program's by a relative error of at most 0.015.
Values may be sent and summed in bfloat16 or wider, within the bound.
A program may use at most 64 MiB of HBM per device.

```python
import jax
import jax.numpy as jnp
from jax import lax

D = 512
HEADS = 8
P_SIZE = 128
NBR = 3
PD = 2
DEV_X = 32
DEV_Y = 16


def device_counts(key):
    first, second = jax.random.split(jax.random.fold_in(key, 11))
    counts = jax.random.randint(first, (DEV_X * DEV_Y,), 1, PD + 1)
    chosen = jax.random.randint(second, (), 0, DEV_X * DEV_Y)
    counts = jnp.where(jnp.arange(DEV_X * DEV_Y) == chosen, PD, counts)
    return counts.reshape(DEV_X, DEV_Y).astype(jnp.int32)


def patch_points(key):
    first, second, third = jax.random.split(jax.random.fold_in(key, 12), 3)
    base = jax.random.randint(first, (DEV_X, DEV_Y, PD), P_SIZE // 4, P_SIZE + 1)
    full_slot = jax.random.randint(second, (DEV_X, DEV_Y, 1), 0, PD)
    slots = jnp.arange(PD)[None, None, :]
    base = jnp.where(slots == full_slot, P_SIZE, base)
    low_device = jax.random.randint(third, (), 0, DEV_X * DEV_Y)
    places = jnp.arange(DEV_X * DEV_Y).reshape(DEV_X, DEV_Y, 1)
    lowest = (places == low_device) & (slots == (full_slot + 1) % PD)
    return jnp.where(lowest, P_SIZE // 4, base).astype(jnp.int32)


def neighbour_codes(key):
    first, second = jax.random.split(jax.random.fold_in(key, 13))
    shape = (DEV_X, DEV_Y, PD, NBR)
    heading = jax.random.randint(first, shape, 1, 5)
    rows = jnp.arange(DEV_X)[:, None, None, None]
    cols = jnp.arange(DEV_Y)[None, :, None, None]
    step_x = jnp.where(heading == 1, -1, jnp.where(heading == 2, 1, 0))
    step_y = jnp.where(heading == 3, -1, jnp.where(heading == 4, 1, 0))
    target_x = rows + step_x
    target_y = cols + step_y
    inside = (target_x >= 0) & (target_x < DEV_X) & (target_y >= 0) & (target_y < DEV_Y)
    heading = jnp.where(inside, heading, 0)
    target_x = jnp.where(inside, target_x, rows + 0 * heading)
    target_y = jnp.where(inside, target_y, cols + 0 * heading)
    counts = device_counts(key)[target_x, target_y]
    slot = jax.random.randint(second, shape, 0, 65536) % counts
    codes = (heading * PD + slot).astype(jnp.int32)
    points = patch_points(key)[target_x, target_y, slot].astype(jnp.int32)
    return (codes, points)


def draw_patch_count(key, part):
    return device_counts(key)


def draw_point_count(key, part):
    return patch_points(key)


def draw_neighbours(key, part):
    return neighbour_codes(key)[0]


def draw_neighbour_points(key, part):
    return neighbour_codes(key)[1]


def draw_feats(key, part):
    shape = (DEV_X, DEV_Y, PD, P_SIZE, D)
    values = jnp.clip(jax.random.normal(key, shape, jnp.float32), -6.0, 6.0)
    return values.astype(jnp.bfloat16)


def base_weights(key):
    first, second = jax.random.split(jax.random.fold_in(key, 31))
    scale = D ** (-0.5)
    primary = jnp.clip(jax.random.normal(first, (D, D), jnp.float32), -5.0, 5.0) * scale
    other = jnp.clip(jax.random.normal(second, (D, D), jnp.float32), -5.0, 5.0) * scale
    return (primary, other)


def draw_w_query(key, part):
    primary, other = base_weights(key)
    return primary.astype(jnp.bfloat16)


def draw_w_key(key, part):
    primary, other = base_weights(key)
    values = other
    return values.astype(jnp.bfloat16)


def block_levels(rng, shape, cuts, least, largest):
    def one(dim, shards_of):
        steps = jax.random.uniform(jax.random.fold_in(jax.random.fold_in(rng, 6), dim), (shards_of,), jnp.float32, least / len(cuts), largest / len(cuts))
        return jnp.repeat(jnp.exp(steps), shape[dim] // shards_of).reshape((-1,) + (1,) * (len(shape) - dim - 1))

    factor_of = one(*cuts[0])
    for cut in cuts[1:]:
        factor_of = factor_of * one(*cut)
    return factor_of


def normal_values(own_key, extent, scale, most, cuts=(), kind=jnp.bfloat16):
    result = jax.random.normal(own_key, extent, jnp.float32) * scale
    if len(cuts) > 0:
        result = block_levels(own_key, extent, cuts, -0.22, 0.18) * result
    return jnp.clip(result, min=-most, max=most).astype(kind)


def setup_inputs(seed: int = 0) -> dict:
    arg_keys = jax.random.split(jax.random.key(seed), 10)
    feats = draw_feats(jax.random.fold_in(arg_keys[9], 71), 0)
    w_query = draw_w_query(jax.random.fold_in(arg_keys[9], 71), 0)
    w_key = draw_w_key(jax.random.fold_in(arg_keys[9], 71), 0)
    w_value = normal_values(arg_keys[3], (D, D), D ** -0.5, 0.25)
    out_grad = normal_values(arg_keys[4], (DEV_X, DEV_Y, PD, P_SIZE, D), 1.0, 6.0, ((0, 32), (1, 16)))
    patch_count = draw_patch_count(jax.random.fold_in(arg_keys[9], 71), 0)
    point_count = draw_point_count(jax.random.fold_in(arg_keys[9], 71), 0)
    neighbours = draw_neighbours(jax.random.fold_in(arg_keys[9], 71), 0)
    neighbour_points = draw_neighbour_points(jax.random.fold_in(arg_keys[9], 71), 0)
    return dict(feats=feats, w_query=w_query, w_key=w_key, w_value=w_value, out_grad=out_grad, patch_count=patch_count, point_count=point_count, neighbours=neighbours, neighbour_points=neighbour_points)


def attend(query, table, codes, key_len, q_valid, grad_out):
    slots, points, width = query.shape
    head_dim = width // HEADS
    scale = head_dim ** -0.5
    high = lax.Precision.HIGHEST
    keys = table.reshape(-1, points, 2 * width)[codes].reshape(slots, -1, 2 * width)
    kk = keys[..., :width].reshape(slots, -1, HEADS, head_dim).astype(jnp.float32)
    vv = keys[..., width:].reshape(slots, -1, HEADS, head_dim)
    vv_f = vv.astype(jnp.float32)
    qq = query.reshape(slots, points, HEADS, head_dim)
    key_valid = (jnp.arange(points, dtype=jnp.int32)[None, None, :] < key_len[:, :, None]).reshape(slots, -1)
    scores = jnp.einsum("sqhd,skhd->shqk", qq.astype(jnp.float32), kk, precision=high) * scale
    scores = jnp.where(key_valid[:, None, None, :], scores, -1e30)
    top = jnp.max(scores, axis=-1, keepdims=True)
    expo = jnp.exp(scores - top)
    probs = expo / jnp.sum(expo, axis=-1, keepdims=True)
    probs_b = probs.astype(jnp.bfloat16)
    mixed = jnp.einsum("shqk,skhd->sqhd", probs_b.astype(jnp.float32), vv_f, precision=high)
    live = q_valid[:, :, None, None]
    out = jnp.where(live, mixed, 0.0).astype(jnp.bfloat16).reshape(slots, points, width)
    grads = grad_out.reshape(slots, points, HEADS, head_dim)
    dout = jnp.where(live, grads, jnp.zeros_like(grads))
    dout_f = dout.astype(jnp.float32)
    dprob = jnp.einsum("sqhd,skhd->shqk", dout_f, vv_f, precision=high)
    inner = jnp.sum(probs * dprob, axis=-1, keepdims=True)
    dscore = (probs * (dprob - inner) * scale).astype(jnp.bfloat16).astype(jnp.float32)
    dquery = jnp.einsum("shqk,skhd->sqhd", dscore, kk, precision=high).astype(jnp.bfloat16).reshape(slots, points, width)
    dkey = jnp.einsum("shqk,sqhd->skhd", dscore, qq.astype(jnp.float32), precision=high)
    dval = jnp.einsum("shqk,sqhd->skhd", probs_b.astype(jnp.float32), dout_f, precision=high)
    contrib = jnp.concatenate([dkey.reshape(-1, points, width), dval.reshape(-1, points, width)], axis=-1)
    contrib = contrib.reshape(contrib.shape[0], -1)
    onehot = (jnp.arange(5 * slots, dtype=jnp.int32)[:, None] == codes.reshape(1, -1)).astype(jnp.float32)
    partial_value = jnp.dot(onehot, contrib, precision=high, preferred_element_type=jnp.float32)
    partial_value = partial_value.astype(jnp.bfloat16).reshape(5, slots, points, 2 * width)
    return out, dquery, partial_value


def reference(feats, w_query, w_key, w_value, out_grad, patch_count, point_count, neighbours, neighbour_points):
    flat = feats.reshape(-1, D)

    def project(weight):
        return jnp.dot(flat, weight, preferred_element_type=jnp.float32).astype(jnp.bfloat16).reshape(feats.shape)

    query = project(w_query)
    keyval = jnp.concatenate([project(w_key), project(w_value)], axis=-1)
    padded = jnp.pad(keyval, ((1, 1), (1, 1), (0, 0), (0, 0), (0, 0)))
    zero = jnp.int32(0)
    offsets = ((1, 1), (0, 1), (2, 1), (1, 0), (1, 2))
    block = (1, 1, PD, P_SIZE, 2 * D)

    def step(total, index):
        row = (index // DEV_Y).astype(jnp.int32)
        col = (index % DEV_Y).astype(jnp.int32)
        table = jnp.stack([lax.dynamic_slice(padded, (row + i, col + j, zero, zero, zero), block)[0, 0] for i, j in offsets])
        own_codes = jnp.concatenate([jnp.arange(PD, dtype=jnp.int32)[:, None], neighbours[row, col]], axis=1)
        counts = point_count[row, col]
        key_len = jnp.concatenate([counts[:, None], neighbour_points[row, col]], axis=1)
        q_valid = (jnp.arange(PD, dtype=jnp.int32)[:, None] < patch_count[row, col]) & (jnp.arange(P_SIZE, dtype=jnp.int32)[None, :] < counts[:, None])
        out, dquery, partial_value = attend(query[row, col], table, own_codes, key_len, q_valid, out_grad[row, col])
        for d, (i, j) in enumerate(offsets):
            start = (row + i, col + j, zero, zero, zero)
            current = lax.dynamic_slice(total, start, block)
            total = lax.dynamic_update_slice(total, current + partial_value[d].astype(jnp.float32)[None, None], start)
        return total, (out, dquery)

    total0 = jnp.zeros(padded.shape, jnp.float32)
    total, (outs, dqueries) = lax.scan(step, total0, jnp.arange(DEV_X * DEV_Y, dtype=jnp.int32))
    grads = total[1:-1, 1:-1].astype(jnp.bfloat16)
    mixed = outs.reshape(feats.shape)
    dq = dqueries.reshape(-1, D)
    dk = grads[..., :D].reshape(-1, D)
    dv = grads[..., D:].reshape(-1, D)
    feat_grad = (jnp.dot(dq, w_query.T, preferred_element_type=jnp.float32)
                 + jnp.dot(dk, w_key.T, preferred_element_type=jnp.float32)
                 + jnp.dot(dv, w_value.T, preferred_element_type=jnp.float32)).astype(jnp.bfloat16).reshape(feats.shape)
    grad_query = jnp.dot(flat.T, dq, preferred_element_type=jnp.float32).astype(jnp.bfloat16)
    grad_key = jnp.dot(flat.T, dk, preferred_element_type=jnp.float32).astype(jnp.bfloat16)
    grad_value = jnp.dot(flat.T, dv, preferred_element_type=jnp.float32).astype(jnp.bfloat16)
    return mixed, feat_grad, grad_query, grad_key, grad_value
```

```python
import functools

import jax
import jax.numpy as jnp
from jax import lax
from jax.experimental import pallas as pl
from jax.experimental.pallas import tpu as pltpu
from jax.sharding import PartitionSpec as P

HEADS = 8
MESH = pl.DeviceIdType.MESH
VMEM_LIMIT = 56 * 1024 * 1024
F32 = jnp.float32
BF16 = jnp.bfloat16

NT = (((1,), (1,)), ((), ()))
TN = (((0,), (0,)), ((), ()))


def dot(a, b, dims=(((1,), (0,)), ((), ()))):
    return lax.dot_general(a, b, dims, preferred_element_type=F32)


def beside():
    a, b = lax.axis_index("gx"), lax.axis_index("gy")
    na, nb = lax.axis_size("gx"), lax.axis_size("gy")
    return (
        ((a + na - 1) % na, b),
        ((a + 1) % na, b),
        (a, (b + nb - 1) % nb),
        (a, (b + 1) % nb),
    )


def greet(peers):
    barrier = pltpu.get_barrier_semaphore()
    for peer in peers:
        pl.semaphore_signal(barrier, inc=1, device_id=peer, device_id_type=MESH)
    pl.semaphore_wait(barrier, len(peers))


def send(src, dst, send_sem, recv_sem, peer):
    copy = pltpu.make_async_remote_copy(
        src_ref=src,
        dst_ref=dst,
        send_sem=send_sem,
        recv_sem=recv_sem,
        device_id=peer,
        device_id_type=MESH,
    )
    copy.start()
    return copy


def halo_kernel(feats, table, own_sem, send_sem, recv_sem):
    peers = beside()
    own = pltpu.make_async_copy(feats, table.at[pl.ds(0, 2)], own_sem)
    own.start()
    greet(peers)
    copies = []
    for d, peer in enumerate(peers):
        back = d ^ 1
        copies.append(
            send(feats, table.at[pl.ds(2 + 2 * back, 2)], send_sem.at[d], recv_sem.at[back], peer)
        )
    own.wait()
    for copy in copies:
        copy.wait()


def halo(feats):
    slots, points, width = feats.shape
    return pl.pallas_call(
        halo_kernel,
        out_shape=jax.ShapeDtypeStruct((5 * slots, points, width), BF16),
        in_specs=[pl.BlockSpec(memory_space=pltpu.VMEM)],
        out_specs=pl.BlockSpec(memory_space=pltpu.VMEM),
        scratch_shapes=[
            pltpu.SemaphoreType.DMA,
            pltpu.SemaphoreType.DMA((4,)),
            pltpu.SemaphoreType.DMA((4,)),
        ],
        compiler_params=pltpu.CompilerParams(
            collective_id=0, has_side_effects=True, vmem_limit_bytes=VMEM_LIMIT
        ),
        name="halo",
    )(feats)


def attend_kernel(
    patch_count, point_count, neighbours, neighbour_points,
    table, w_query, w_key, w_value, out_grad,
    mixed, own_grad, far_grad, grads,
    rows, keys, values, query, dquery, dkeys, dvalues, total,
):
    slots, points, width = out_grad.shape
    near = neighbours.shape[-1]
    per = (near + 1) * points
    lane = lax.broadcasted_iota(jnp.int32, (points, 128), 1)
    low = lane < 64
    codes = []
    for s in range(slots):
        for m in range(near + 1):
            code = s if m == 0 else neighbours[0, 0, s, m - 1]
            codes.append(code)
            rows[pl.ds((s * (near + 1) + m) * points, points), :] = table[code]
    for s in range(slots):
        query[pl.ds(s * points, points), :] = dot(table[s], w_query[...]).astype(BF16)
    for s in range(slots):
        part = pl.ds(s * per, per)
        keys[part, :] = dot(rows[part, :], w_key[...]).astype(BF16)
        values[part, :] = dot(rows[part, :], w_value[...]).astype(BF16)

    for s in range(slots):
        part = pl.ds(s * per, per)
        count = jnp.where(s < patch_count[0, 0], point_count[0, 0, s], 0)
        live = lax.broadcasted_iota(jnp.int32, (points, 128), 0) < count
        bias = []
        for m in range(near + 1):
            most = point_count[0, 0, s] if m == 0 else neighbour_points[0, 0, s, m - 1]
            dead = lax.broadcasted_iota(jnp.int32, (points, 128), 0) >= most
            bias.append(jnp.where(dead & (lane == 0), -1e30, 0.0).astype(BF16))
        bias = jnp.concatenate(bias, axis=0)
        one = jnp.where(lax.broadcasted_iota(jnp.int32, (2 * points, 128), 1) == 0, 1.0, 0.0).astype(BF16)
        for pair in range(width // 128):
            lanes = pl.ds(pair * 128, 128)
            kk = keys[part, lanes]
            vv = values[part, lanes]
            qq = query[pl.ds(s * points, points), lanes].astype(F32) * 0.125
            gg = jnp.where(live, out_grad[s, :, lanes].astype(F32), 0.0)
            qq = jnp.concatenate([jnp.where(low, qq, 0.0), jnp.where(low, 0.0, qq)], axis=0).astype(BF16)
            gg = jnp.concatenate([jnp.where(low, gg, 0.0), jnp.where(low, 0.0, gg)], axis=0).astype(BF16)
            score = dot(jnp.concatenate([kk, bias], axis=1), jnp.concatenate([qq, one], axis=1), NT)
            dprob = dot(vv, gg, NT)
            top = jnp.max(score, axis=0, keepdims=True)
            expo = jnp.exp(score - top)
            inverse = 1.0 / jnp.sum(expo, axis=0, keepdims=True)
            prob = expo * inverse
            inner = jnp.sum(prob * dprob, axis=0, keepdims=True)
            dscore = (prob * (dprob - inner)).astype(BF16)
            prob = prob.astype(BF16)
            out = dot(vv, prob, TN)
            dq = dot(kk, dscore, TN)
            top_half = lax.broadcasted_iota(jnp.int32, (128, points), 0) < 64
            out = jnp.where(top_half, out[:, :points], out[:, points:]).T
            dq = jnp.where(top_half, dq[:, :points], dq[:, points:]).T
            mixed[s, :, lanes] = jnp.where(live, out, 0.0).astype(BF16)
            dquery[pl.ds(s * points, points), lanes] = (dq * 0.125).astype(BF16)
            dkeys[part, lanes] = dot(dscore, qq).astype(BF16)
            dvalues[part, lanes] = dot(prob, gg).astype(BF16)

    total[...] = jnp.zeros_like(total)
    for s in range(slots):
        part = pl.ds(s * per, per)
        term = dot(dkeys[part, :], w_key[...], NT) + dot(dvalues[part, :], w_value[...], NT)
        total[s] += dot(dquery[pl.ds(s * points, points), :], w_query[...], NT)
        for m in range(near + 1):
            code = codes[s * (near + 1) + m]
            total[code] += term[m * points : (m + 1) * points]
    own_grad[...] = total[pl.ds(0, slots)]
    far_grad[...] = total[pl.ds(slots, 4 * slots)].astype(BF16)
    own = table[pl.ds(0, slots)].reshape(slots * points, width)
    grads[:, :width] = dot(own, dquery[...], TN).astype(BF16)
    grads[:, width : 2 * width] = dot(rows[...], dkeys[...], TN).astype(BF16)
    grads[:, 2 * width :] = dot(rows[...], dvalues[...], TN).astype(BF16)


def attend(patch_count, point_count, neighbours, neighbour_points, table, w_query, w_key, w_value, out_grad):
    slots, points, width = out_grad.shape
    entries = slots * (neighbours.shape[-1] + 1) * points
    smem = pl.BlockSpec(memory_space=pltpu.SMEM)
    vmem = pl.BlockSpec(memory_space=pltpu.VMEM)
    return pl.pallas_call(
        attend_kernel,
        out_shape=[
            jax.ShapeDtypeStruct((slots, points, width), BF16),
            jax.ShapeDtypeStruct((slots, points, width), F32),
            jax.ShapeDtypeStruct((4 * slots, points, width), BF16),
            jax.ShapeDtypeStruct((width, 3 * width), BF16),
        ],
        in_specs=[smem] * 4 + [vmem] * 5,
        out_specs=[vmem] * 4,
        scratch_shapes=[
            pltpu.VMEM((entries, width), BF16),
            pltpu.VMEM((entries, width), BF16),
            pltpu.VMEM((entries, width), BF16),
            pltpu.VMEM((slots * points, width), BF16),
            pltpu.VMEM((slots * points, width), BF16),
            pltpu.VMEM((entries, width), BF16),
            pltpu.VMEM((entries, width), BF16),
            pltpu.VMEM((5 * slots, points, width), F32),
        ],
        compiler_params=pltpu.CompilerParams(vmem_limit_bytes=VMEM_LIMIT),
        name="attend",
    )(patch_count, point_count, neighbours, neighbour_points, table, w_query, w_key, w_value, out_grad)


def reduce_kernel(
    own_grad, far_grad, grads,
    feat_grad, summed,
    back, from_core, half, from1, part1, from2, part2, from3, whole3,
    s_back, r_back, s_core, r_core, s1, r1, s2, r2, s3, r3, s4, r4, s5, r5, s6, r6, s7, r7,
):
    a, b = lax.axis_index("gx"), lax.axis_index("gy")
    core, x, zh = a % 2, (a // 2) % 4, a // 8
    y, zl = b // 4, b % 4
    z = zh * 4 + zl
    wide = grads.shape[1]

    def device(core_=core, x_=x, y_=y, z_=z):
        return ((z_ // 4 * 4 + x_) * 2 + core_, y_ * 4 + z_ % 4)

    sides = beside()
    partner = device(core_=1 - core)
    xs = [(x + k) % 4 for k in range(1, 4)]
    ys = [(y + k) % 4 for k in range(1, 4)]
    zs = [(z + k) % 16 for k in range(1, 16)]
    x_devices = [device(x_=i) for i in xs]
    y_devices = [device(y_=i) for i in ys]
    z_devices = [device(z_=i) for i in zs]
    greet([*sides, partner, *x_devices, *y_devices, *z_devices])

    swap = send(grads.at[pl.ds((1 - core) * 256, 256)], from_core, s_core, r_core, partner)
    returns = [
        send(far_grad.at[pl.ds(2 * d, 2)], back.at[d ^ 1], s_back.at[d], r_back.at[d ^ 1], peer)
        for d, peer in enumerate(sides)
    ]
    swap.wait()
    half[...] = (
        grads[pl.ds(core * 256, 256), :].astype(F32) + from_core[...].astype(F32)
    ).astype(BF16)

    orders = ((x, xs, x_devices, y, ys, y_devices), (y, ys, y_devices, x, xs, x_devices))
    copies = []
    for h, (me, others, devices, _, _, _) in enumerate(orders):
        for k in range(3):
            copies.append(
                send(
                    half.at[pl.ds(h * 128 + others[k] * 32, 32)],
                    from1.at[h, k],
                    s1.at[h, k],
                    r1.at[h, k],
                    devices[k],
                )
            )
    for h, (me, others, devices, _, _, _) in enumerate(orders):
        for k in range(3):
            copies[3 * h + k].wait()
        acc = half[pl.ds(h * 128 + me * 32, 32), :].astype(F32)
        for k in range(3):
            acc = acc + from1[h, k].astype(F32)
        part1[h] = acc.astype(BF16)

    copies = []
    for h, (_, _, _, me, others, devices) in enumerate(orders):
        for k in range(3):
            i = others[k]
            copies.append(
                send(
                    part1.at[h, pl.ds(i // 2 * 16, 16), pl.ds(i % 2 * 768, 768)],
                    from2.at[h, k],
                    s2.at[h, k],
                    r2.at[h, k],
                    devices[k],
                )
            )
    for h, (_, _, _, me, others, devices) in enumerate(orders):
        for k in range(3):
            copies[3 * h + k].wait()
        acc = part1[h, pl.ds(me // 2 * 16, 16), pl.ds(me % 2 * 768, 768)].astype(F32)
        for k in range(3):
            acc = acc + from2[h, k].astype(F32)
        acc = acc.astype(BF16)
        for t in range(6):
            part2[6 * h + t] = acc[:, t * 128 : (t + 1) * 128]
    part2[pl.ds(12, 4)] = jnp.zeros((4, 16, 128), BF16)

    copies = [
        send(part2.at[zs[k]], from3.at[k], s3.at[k], r3.at[k], z_devices[k]) for k in range(15)
    ]
    acc = part2[z].astype(F32)
    for k in range(15):
        copies[k].wait()
        acc = acc + from3[k].astype(F32)
    whole3[z] = acc.astype(BF16)

    copies = [
        send(whole3.at[z], whole3.at[z], s4.at[k], r4.at[k], z_devices[k]) for k in range(15)
    ]
    for copy in copies:
        copy.wait()

    def piece(h, first, second):
        rows = core * 256 + h * 128 + first * 32 + second // 2 * 16
        return summed.at[pl.ds(rows, 16), pl.ds(second % 2 * 768, 768)]

    copies = []
    for h, (first, _, _, second, others, devices) in enumerate(orders):
        mine = piece(h, first, second)
        mine[...] = jnp.concatenate([whole3[6 * h + t] for t in range(6)], axis=1)
        for k in range(3):
            copies.append(send(mine, mine, s5.at[h, k], r5.at[h, k], devices[k]))
    for copy in copies:
        copy.wait()
    copies = []
    for h, (first, others, devices, _, _, _) in enumerate(orders):
        mine = summed.at[pl.ds(core * 256 + h * 128 + first * 32, 32)]
        for k in range(3):
            copies.append(send(mine, mine, s6.at[h, k], r6.at[h, k], devices[k]))
    for copy in copies:
        copy.wait()
    mine = summed.at[pl.ds(core * 256, 256)]
    swap = send(mine, mine, s7, r7, partner)

    for copy in returns:
        copy.wait()
    acc = own_grad[...]
    for d in range(4):
        acc = acc + back[d].astype(F32)
    feat_grad[...] = acc.astype(BF16)
    swap.wait()


def reduce(own_grad, far_grad, grads):
    slots, points, width = own_grad.shape
    dma = pltpu.SemaphoreType.DMA
    vmem = pl.BlockSpec(memory_space=pltpu.VMEM)
    return pl.pallas_call(
        reduce_kernel,
        out_shape=[
            jax.ShapeDtypeStruct((slots, points, width), BF16),
            jax.ShapeDtypeStruct((width, 3 * width), BF16),
        ],
        in_specs=[vmem] * 3,
        out_specs=[vmem] * 2,
        scratch_shapes=[
            pltpu.VMEM((4, slots, points, width), BF16),
            pltpu.VMEM((256, 1536), BF16),
            pltpu.VMEM((256, 1536), BF16),
            pltpu.VMEM((2, 3, 32, 1536), BF16),
            pltpu.VMEM((2, 32, 1536), BF16),
            pltpu.VMEM((2, 3, 16, 768), BF16),
            pltpu.VMEM((16, 16, 128), BF16),
            pltpu.VMEM((15, 16, 128), BF16),
            pltpu.VMEM((16, 16, 128), BF16),
            dma((4,)), dma((4,)),
            dma, dma,
            dma((2, 3)), dma((2, 3)),
            dma((2, 3)), dma((2, 3)),
            dma((15,)), dma((15,)),
            dma((15,)), dma((15,)),
            dma((2, 3)), dma((2, 3)),
            dma((2, 3)), dma((2, 3)),
            dma, dma,
        ],
        compiler_params=pltpu.CompilerParams(
            collective_id=1, has_side_effects=True, vmem_limit_bytes=VMEM_LIMIT
        ),
        name="reduce",
    )(own_grad, far_grad, grads)


def body(
    feats, w_query, w_key, w_value, out_grad, patch_count, point_count, neighbours, neighbour_points
):
    slots, points, width = (feats.shape[2], feats.shape[3], feats.shape[4])
    own = feats.reshape(slots, points, width)
    table = halo(own)
    mixed, own_grad, far_grad, grads = attend(
        patch_count, point_count, neighbours, neighbour_points,
        table, w_query, w_key, w_value, out_grad.reshape(slots, points, width),
    )
    feat_grad, summed = reduce(own_grad, far_grad, grads)
    return (
        mixed.reshape(feats.shape),
        feat_grad.reshape(feats.shape),
        summed[:, :width],
        summed[:, width : 2 * width],
        summed[:, 2 * width :],
    )


def solution(mesh):
    return jax.shard_map(
        body,
        mesh=mesh,
        in_specs=(
            P("gx", "gy", None, None, None),
            P(),
            P(),
            P(),
            P("gx", "gy", None, None, None),
            P("gx", "gy"),
            P("gx", "gy", None),
            P("gx", "gy", None, None),
            P("gx", "gy", None, None),
        ),
        out_specs=(P("gx", "gy", None, None, None), P("gx", "gy", None, None, None), P(), P(), P()),
        check_vma=False,
    )
```

```python
import functools

import jax
import jax.numpy as jnp
from jax import lax
from jax.experimental import pallas as pl
from jax.experimental.pallas import tpu as pltpu
from jax.sharding import PartitionSpec as P

HEADS = 8
MESH = pl.DeviceIdType.MESH
VMEM_LIMIT = 56 * 1024 * 1024
F32 = jnp.float32
BF16 = jnp.bfloat16

NT = (((1,), (1,)), ((), ()))
TN = (((0,), (0,)), ((), ()))


def dot(a, b, dims=(((1,), (0,)), ((), ()))):
    return lax.dot_general(a, b, dims, preferred_element_type=F32)


def send(src, dst, send_sem, recv_sem, peer):
    copy = pltpu.make_async_remote_copy(
        src_ref=src,
        dst_ref=dst,
        send_sem=send_sem,
        recv_sem=recv_sem,
        device_id=peer,
        device_id_type=MESH,
    )
    copy.start()
    return copy


class Place:
    def __init__(self):
        a, b = lax.axis_index("gx"), lax.axis_index("gy")
        self.core, self.x, self.zh, self.y, self.zl = a % 2, (a // 2) % 4, a // 8, b // 4, b % 4
        self.other = 1 - self.core
        self.edge = self.x == 3 * self.core
        self.partner = self.at(core=self.other)
        self.outer = ((a + 31 + 2 * self.core) % 32, b)
        self.down, self.up = (a, (b + 15) % 16), (a, (b + 1) % 16)
        self.source = self.at(x=3 * self.core)
        self.final = self.at(core=self.other, x=3 * self.other, zh=(self.zh + 3 + 2 * self.core) % 4)
        self.reached = [
            self.at(core=self.other, x=p, zh=(self.zh + 3 + 2 * self.core) % 4) for p in range(4)
        ]
        self.turn = [(self.x + k) % 4 for k in range(1, 4)]

    def at(self, core=None, x=None, zh=None, y=None, zl=None):
        core = self.core if core is None else core
        x = self.x if x is None else x
        zh = self.zh if zh is None else zh
        y = self.y if y is None else y
        zl = self.zl if zl is None else zl
        return ((zh * 4 + x) * 2 + core, y * 4 + zl)


def signal(peers):
    barrier = pltpu.get_barrier_semaphore()
    for peer in peers:
        pl.semaphore_signal(barrier, inc=1, device_id=peer, device_id_type=MESH)


def greet(here, peers):
    barrier = pltpu.get_barrier_semaphore()
    peers = [here.partner, here.down, here.up, *peers]
    signal(peers)

    @pl.when(here.edge)
    def _():
        signal([here.at(x=p) for p in here.turn] + here.reached)
        pl.semaphore_wait(barrier, len(peers) + 7)

    @pl.when(jnp.logical_not(here.edge))
    def _():
        signal([here.source, here.final, here.outer])
        pl.semaphore_wait(barrier, len(peers) + 3)


def quarter(ref, p):
    return ref.at[p // 2, pl.ds(p % 2 * 64, 64)]


def flat_wait(ref, sem):
    pltpu.make_async_copy(ref, ref, sem).wait()


EXCHANGE_SCRATCH = [
    pltpu.VMEM((64, 512), BF16),
    pltpu.SemaphoreType.DMA((4,)),
    pltpu.SemaphoreType.DMA((4,)),
    pltpu.SemaphoreType.DMA((4,)),
    pltpu.SemaphoreType.DMA((4,)),
    pltpu.SemaphoreType.DMA((2,)),
]


def exchange_start(here, src, dst, relay, s, r, sq, rq, hop):
    @pl.when(here.edge)
    def _():
        for p in here.turn:
            send(quarter(src[1], p), relay, sq.at[p], hop.at[0], here.at(x=p))
        send(quarter(src[1], here.x), quarter(dst[1], here.x), sq.at[here.x], rq.at[here.x], here.final)

    send(src[3], dst[2], s.at[3], r.at[2], here.up)
    send(src[2], dst[3], s.at[2], r.at[3], here.down)
    send(src[0], dst[0], s.at[0], r.at[0], here.partner)

    @pl.when(jnp.logical_not(here.edge))
    def _():
        send(src[1], dst[1], s.at[1], r.at[1], here.outer)


def exchange_relay(here, src, dst, relay, s, r, sq, rq, hop):
    @pl.when(jnp.logical_not(here.edge))
    def _():
        flat_wait(relay, hop.at[0])
        send(relay, quarter(dst[1], here.x), hop.at[1], rq.at[here.x], here.final)


def exchange_finish(here, src, dst, relay, s, r, sq, rq, hop):
    for d in (0, 2, 3):
        flat_wait(dst[d], r.at[d])

    @pl.when(here.edge)
    def _():
        for p in range(4):
            flat_wait(relay, rq.at[p])
        for p in range(4):
            flat_wait(relay, sq.at[p])

    @pl.when(jnp.logical_not(here.edge))
    def _():
        flat_wait(dst[1], r.at[1])
        flat_wait(src[1], s.at[1])
        flat_wait(relay, hop.at[1])

    for d in (0, 2, 3):
        flat_wait(src[d], s.at[d])


def halo_kernel(feats, table, own_sem, *scratch):
    here = Place()
    own = pltpu.make_async_copy(feats, table.at[pl.ds(0, 2)], own_sem)
    own.start()
    greet(here, [])
    src = [feats] * 4
    dst = [table.at[pl.ds(2 + 2 * d, 2)] for d in range(4)]
    exchange_start(here, src, dst, *scratch)
    exchange_relay(here, src, dst, *scratch)
    own.wait()
    exchange_finish(here, src, dst, *scratch)


def halo(feats):
    slots, points, width = feats.shape
    return pl.pallas_call(
        halo_kernel,
        out_shape=jax.ShapeDtypeStruct((5 * slots, points, width), BF16),
        in_specs=[pl.BlockSpec(memory_space=pltpu.VMEM)],
        out_specs=pl.BlockSpec(memory_space=pltpu.VMEM),
        scratch_shapes=[pltpu.SemaphoreType.DMA, *EXCHANGE_SCRATCH],
        compiler_params=pltpu.CompilerParams(
            collective_id=0, has_side_effects=True, vmem_limit_bytes=VMEM_LIMIT
        ),
        name="halo",
    )(feats)


def side_of(code, even):
    swapped = jnp.where(code < 4, code + 2, code - 2)
    return jnp.where(even & (code >= 2) & (code < 6), swapped, code)


def attend_kernel(
    patch_count, point_count, neighbours, neighbour_points,
    table, w_query, w_key, w_value, out_grad,
    mixed, own_grad, far_grad, grads,
    rows, keys, values, query, dquery, dkeys, dvalues, total,
):
    slots, points, width = out_grad.shape
    near = neighbours.shape[-1]
    per = (near + 1) * points
    lane = lax.broadcasted_iota(jnp.int32, (points, 128), 1)
    low = lane < 64
    even = lax.axis_index("gx") % 2 == 0
    codes = []
    for s in range(slots):
        for m in range(near + 1):
            code = s if m == 0 else side_of(neighbours[0, 0, s, m - 1], even)
            codes.append(code)
            rows[pl.ds((s * (near + 1) + m) * points, points), :] = table[code]
    for s in range(slots):
        query[pl.ds(s * points, points), :] = dot(table[s], w_query[...]).astype(BF16)
    for s in range(slots):
        part = pl.ds(s * per, per)
        keys[part, :] = dot(rows[part, :], w_key[...]).astype(BF16)
        values[part, :] = dot(rows[part, :], w_value[...]).astype(BF16)

    for s in range(slots):
        part = pl.ds(s * per, per)
        count = jnp.where(s < patch_count[0, 0], point_count[0, 0, s], 0)
        live = lax.broadcasted_iota(jnp.int32, (points, 128), 0) < count
        bias = []
        for m in range(near + 1):
            most = point_count[0, 0, s] if m == 0 else neighbour_points[0, 0, s, m - 1]
            dead = lax.broadcasted_iota(jnp.int32, (points, 128), 0) >= most
            bias.append(jnp.where(dead & (lane == 0), -1e30, 0.0).astype(BF16))
        bias = jnp.concatenate(bias, axis=0)
        one = jnp.where(lax.broadcasted_iota(jnp.int32, (2 * points, 128), 1) == 0, 1.0, 0.0).astype(BF16)
        for pair in range(width // 128):
            lanes = pl.ds(pair * 128, 128)
            kk = keys[part, lanes]
            vv = values[part, lanes]
            qq = query[pl.ds(s * points, points), lanes].astype(F32) * 0.125
            gg = jnp.where(live, out_grad[s, :, lanes].astype(F32), 0.0)
            qq = jnp.concatenate([jnp.where(low, qq, 0.0), jnp.where(low, 0.0, qq)], axis=0).astype(BF16)
            gg = jnp.concatenate([jnp.where(low, gg, 0.0), jnp.where(low, 0.0, gg)], axis=0).astype(BF16)
            score = dot(jnp.concatenate([kk, bias], axis=1), jnp.concatenate([qq, one], axis=1), NT)
            dprob = dot(vv, gg, NT)
            top = jnp.max(score, axis=0, keepdims=True)
            expo = jnp.exp(score - top)
            inverse = 1.0 / jnp.sum(expo, axis=0, keepdims=True)
            prob = expo * inverse
            inner = jnp.sum(prob * dprob, axis=0, keepdims=True)
            dscore = (prob * (dprob - inner)).astype(BF16)
            prob = prob.astype(BF16)
            out = dot(vv, prob, TN)
            dq = dot(kk, dscore, TN)
            top_half = lax.broadcasted_iota(jnp.int32, (128, points), 0) < 64
            out = jnp.where(top_half, out[:, :points], out[:, points:]).T
            dq = jnp.where(top_half, dq[:, :points], dq[:, points:]).T
            mixed[s, :, lanes] = jnp.where(live, out, 0.0).astype(BF16)
            dquery[pl.ds(s * points, points), lanes] = (dq * 0.125).astype(BF16)
            dkeys[part, lanes] = dot(dscore, qq).astype(BF16)
            dvalues[part, lanes] = dot(prob, gg).astype(BF16)

    total[...] = jnp.zeros_like(total)
    for s in range(slots):
        part = pl.ds(s * per, per)
        term = dot(dkeys[part, :], w_key[...], NT) + dot(dvalues[part, :], w_value[...], NT)
        total[s] += dot(dquery[pl.ds(s * points, points), :], w_query[...], NT)
        for m in range(near + 1):
            code = codes[s * (near + 1) + m]
            total[code] += term[m * points : (m + 1) * points]
    own_grad[...] = total[pl.ds(0, slots)]
    far_grad[...] = total[pl.ds(slots, 4 * slots)].astype(BF16)
    own = table[pl.ds(0, slots)].reshape(slots * points, width)
    grads[:, :width] = dot(own, dquery[...], TN).astype(BF16)
    grads[:, width : 2 * width] = dot(rows[...], dkeys[...], TN).astype(BF16)
    grads[:, 2 * width :] = dot(rows[...], dvalues[...], TN).astype(BF16)


def attend(patch_count, point_count, neighbours, neighbour_points, table, w_query, w_key, w_value, out_grad):
    slots, points, width = out_grad.shape
    entries = slots * (neighbours.shape[-1] + 1) * points
    smem = pl.BlockSpec(memory_space=pltpu.SMEM)
    vmem = pl.BlockSpec(memory_space=pltpu.VMEM)
    return pl.pallas_call(
        attend_kernel,
        out_shape=[
            jax.ShapeDtypeStruct((slots, points, width), BF16),
            jax.ShapeDtypeStruct((slots, points, width), F32),
            jax.ShapeDtypeStruct((4 * slots, points, width), BF16),
            jax.ShapeDtypeStruct((width, 3 * width), BF16),
        ],
        in_specs=[smem] * 4 + [vmem] * 5,
        out_specs=[vmem] * 4,
        scratch_shapes=[
            pltpu.VMEM((entries, width), BF16),
            pltpu.VMEM((entries, width), BF16),
            pltpu.VMEM((entries, width), BF16),
            pltpu.VMEM((slots * points, width), BF16),
            pltpu.VMEM((slots * points, width), BF16),
            pltpu.VMEM((entries, width), BF16),
            pltpu.VMEM((entries, width), BF16),
            pltpu.VMEM((5 * slots, points, width), F32),
        ],
        compiler_params=pltpu.CompilerParams(vmem_limit_bytes=VMEM_LIMIT),
        name="attend",
    )(patch_count, point_count, neighbours, neighbour_points, table, w_query, w_key, w_value, out_grad)


RETURN_AT = 4


def reduce_kernel(
    far_grad, grads,
    back, summed,
    from0, half, from1, part1, from2, part2, from3, from4, whole,
    s0, r0, s1, r1, s2, r2, s3, r3, s4, r4, s5, r5, s6, r6, s7, r7, s8, r8,
    *scratch,
):
    here = Place()
    core, x, y, zh, zl = here.core, here.x, here.y, here.zh, here.zl
    xs, ys, hs, ls = ([(i + k) % 4 for k in range(1, 4)] for i in (x, y, zh, zl))
    x_devices = [here.at(x=i) for i in xs]
    y_devices = [here.at(y=i) for i in ys]
    h_devices = [here.at(zh=i) for i in hs]
    l_devices = [here.at(zl=i) for i in ls]
    greet(here, [*x_devices, *y_devices, *h_devices, *l_devices])
    src = [far_grad.at[pl.ds(2 * d, 2)] for d in range(4)]
    dst = [back.at[d] for d in range(4)]

    def returns(at):
        if at == RETURN_AT:
            exchange_start(here, src, dst, *scratch)
        if at == RETURN_AT + 1:
            exchange_relay(here, src, dst, *scratch)

    orders = ((x, xs, x_devices, y, ys, y_devices), (y, ys, y_devices, x, xs, x_devices))
    pieces = [(h, k) for k in range(3) for h in range(2)] + [(0, 3), (1, 3)]

    def row_of(h, k):
        return h * 128 + (orders[h][1][k] if k < 3 else orders[h][0]) * 32

    swaps = []
    for n, (h, k) in enumerate(pieces):
        row = row_of(h, k)
        swaps.append(
            send(
                grads.at[pl.ds(here.other * 256 + row, 32)],
                from0.at[pl.ds(row, 32)],
                s0.at[n],
                r0.at[n],
                here.partner,
            )
        )
    returns(0)
    first = {}
    for n, (h, k) in enumerate(pieces):
        row = row_of(h, k)
        swaps[n].wait_recv()
        acc = grads[pl.ds(core * 256 + row, 32), :].astype(F32) + from0[pl.ds(row, 32), :].astype(F32)
        half[pl.ds(row, 32), :] = acc.astype(BF16)
        if k < 3:
            first[h, k] = send(
                half.at[pl.ds(row, 32)], from1.at[h, k], s1.at[h, k], r1.at[h, k], orders[h][2][k]
            )
    returns(1)
    second = {}
    for h, (me, _, _, _, others, devices) in enumerate(orders):
        acc = half[pl.ds(h * 128 + me * 32, 32), :].astype(F32)
        for k in range(3):
            first[h, k].wait_recv()
            acc = acc + from1[h, k].astype(F32)
        part1[h] = acc.astype(BF16)
        for k in range(3):
            i = others[k]
            second[h, k] = send(
                part1.at[h, pl.ds(i // 2 * 16, 16), pl.ds(i % 2 * 768, 768)],
                from2.at[h, k],
                s2.at[h, k],
                r2.at[h, k],
                devices[k],
            )
    part2[pl.ds(12, 4)] = jnp.zeros((4, 16, 128), BF16)
    returns(2)
    for h, (_, _, _, me, _, _) in enumerate(orders):
        acc = part1[h, pl.ds(me // 2 * 16, 16), pl.ds(me % 2 * 768, 768)].astype(F32)
        for k in range(3):
            second[h, k].wait_recv()
            acc = acc + from2[h, k].astype(F32)
        acc = acc.astype(BF16)
        for t in range(6):
            part2[6 * h + t] = acc[:, t * 128 : (t + 1) * 128]

    third = [
        send(part2.at[pl.ds(ls[k] * 4, 4)], from3.at[k], s3.at[k], r3.at[k], l_devices[k])
        for k in range(3)
    ]
    acc = part2[pl.ds(zl * 4, 4)].astype(F32)
    for k in range(3):
        third[k].wait_recv()
        acc = acc + from3[k].astype(F32)
    from4[zh] = acc.astype(BF16)
    fourth = [
        send(from4.at[zh], from4.at[zh], s4.at[k], r4.at[k], h_devices[k]) for k in range(3)
    ]
    returns(3)
    for k in range(3):
        fourth[k].wait_recv()
    acc = from4[0].astype(F32)
    for i in range(1, 4):
        acc = acc + from4[i].astype(F32)
    mine = whole.at[pl.ds(zl * 4, 4)]
    mine[...] = acc.astype(BF16)
    fifth = [send(mine, mine, s5.at[k], r5.at[k], l_devices[k]) for k in range(3)]
    returns(4)
    for k in range(3):
        fifth[k].wait_recv()

    sixth = {}
    for h, (me, _, _, place, _, devices) in enumerate(orders):
        mine = summed.at[
            pl.ds(core * 256 + h * 128 + me * 32 + place // 2 * 16, 16), pl.ds(place % 2 * 768, 768)
        ]
        mine[...] = jnp.concatenate([whole[6 * h + t] for t in range(6)], axis=1)
        for k in range(3):
            sixth[h, k] = send(mine, mine, s6.at[h, k], r6.at[h, k], devices[k])
    returns(5)
    seventh, eighth = {}, []
    for h, (me, _, devices, _, _, _) in enumerate(orders):
        for k in range(3):
            sixth[h, k].wait_recv()
        mine = summed.at[pl.ds(core * 256 + h * 128 + me * 32, 32)]
        for k in range(3):
            seventh[h, k] = send(mine, mine, s7.at[h, k], r7.at[h, k], devices[k])
        eighth.append(send(mine, mine, s8.at[h, 3], r8.at[h, 3], here.partner))
    for k in (0, 2, 1):
        for h, (me, _, _, _, _, _) in enumerate(orders):
            seventh[h, k].wait_recv()
            mine = summed.at[pl.ds(core * 256 + h * 128 + (me + 3 - k) % 4 * 32, 32)]
            eighth.append(send(mine, mine, s8.at[h, k], r8.at[h, k], here.partner))
    exchange_finish(here, src, dst, *scratch)
    for copy in eighth:
        copy.wait()
    for copy in [
        *swaps, *first.values(), *second.values(), *third, *fourth, *fifth,
        *sixth.values(), *seventh.values(),
    ]:
        copy.wait_send()


def reduce(far_grad, grads):
    slots, points, width = far_grad.shape
    dma = pltpu.SemaphoreType.DMA
    vmem = pl.BlockSpec(memory_space=pltpu.VMEM)
    return pl.pallas_call(
        reduce_kernel,
        out_shape=[
            jax.ShapeDtypeStruct((4, slots // 4, points, width), BF16),
            jax.ShapeDtypeStruct((width, 3 * width), BF16),
        ],
        in_specs=[vmem] * 2,
        out_specs=[vmem] * 2,
        scratch_shapes=[
            pltpu.VMEM((256, 1536), BF16),
            pltpu.VMEM((256, 1536), BF16),
            pltpu.VMEM((2, 3, 32, 1536), BF16),
            pltpu.VMEM((2, 32, 1536), BF16),
            pltpu.VMEM((2, 3, 16, 768), BF16),
            pltpu.VMEM((16, 16, 128), BF16),
            pltpu.VMEM((3, 4, 16, 128), BF16),
            pltpu.VMEM((4, 4, 16, 128), BF16),
            pltpu.VMEM((16, 16, 128), BF16),
            dma((8,)), dma((8,)),
            dma((2, 3)), dma((2, 3)),
            dma((2, 3)), dma((2, 3)),
            dma((3,)), dma((3,)),
            dma((3,)), dma((3,)),
            dma((3,)), dma((3,)),
            dma((2, 3)), dma((2, 3)),
            dma((2, 3)), dma((2, 3)),
            dma((2, 4)), dma((2, 4)),
            *EXCHANGE_SCRATCH,
        ],
        compiler_params=pltpu.CompilerParams(
            collective_id=1, has_side_effects=True, vmem_limit_bytes=VMEM_LIMIT
        ),
        name="reduce",
    )(far_grad, grads)


def finish_kernel(own_grad, back, summed, feat_grad, *parts):
    acc = own_grad[...]
    for d in range(4):
        acc = acc + back[d].astype(F32)
    feat_grad[...] = acc.astype(BF16)
    width = parts[0].shape[1]
    for i, part in enumerate(parts):
        part[...] = summed[:, i * width : (i + 1) * width]


def finish(own_grad, back, summed):
    vmem = pl.BlockSpec(memory_space=pltpu.VMEM)
    width = summed.shape[0]
    return pl.pallas_call(
        finish_kernel,
        out_shape=[jax.ShapeDtypeStruct(own_grad.shape, BF16)]
        + [jax.ShapeDtypeStruct((width, width), BF16)] * 3,
        in_specs=[vmem] * 3,
        out_specs=[vmem] * 4,
        compiler_params=pltpu.CompilerParams(vmem_limit_bytes=VMEM_LIMIT),
        name="finish",
    )(own_grad, back, summed)


def body(
    feats, w_query, w_key, w_value, out_grad, patch_count, point_count, neighbours, neighbour_points
):
    slots, points, width = (feats.shape[2], feats.shape[3], feats.shape[4])
    own = feats.reshape(slots, points, width)
    table = halo(own)
    mixed, own_grad, far_grad, grads = attend(
        patch_count, point_count, neighbours, neighbour_points,
        table, w_query, w_key, w_value, out_grad.reshape(slots, points, width),
    )
    back, summed = reduce(far_grad, grads)
    feat_grad, *sums = finish(own_grad, back, summed)
    return (mixed.reshape(feats.shape), feat_grad.reshape(feats.shape), *sums)


def solution(mesh):
    return jax.shard_map(
        body,
        mesh=mesh,
        in_specs=(
            P("gx", "gy", None, None, None),
            P(),
            P(),
            P(),
            P("gx", "gy", None, None, None),
            P("gx", "gy"),
            P("gx", "gy", None),
            P("gx", "gy", None, None),
            P("gx", "gy", None, None),
        ),
        out_specs=(P("gx", "gy", None, None, None), P("gx", "gy", None, None, None), P(), P(), P()),
        check_vma=False,
    )
```

```python
import functools

import jax
import jax.numpy as jnp
from jax import lax
from jax.experimental import pallas as pl
from jax.experimental.pallas import tpu as pltpu
from jax.sharding import PartitionSpec as P

HEADS = 8
MESH = pl.DeviceIdType.MESH
VMEM_LIMIT = 56 * 1024 * 1024
F32 = jnp.float32
BF16 = jnp.bfloat16

NT = (((1,), (1,)), ((), ()))
TN = (((0,), (0,)), ((), ()))


def dot(a, b, dims=(((1,), (0,)), ((), ()))):
    return lax.dot_general(a, b, dims, preferred_element_type=F32)


def send(src, dst, send_sem, recv_sem, peer):
    copy = pltpu.make_async_remote_copy(
        src_ref=src,
        dst_ref=dst,
        send_sem=send_sem,
        recv_sem=recv_sem,
        device_id=peer,
        device_id_type=MESH,
    )
    copy.start()
    return copy


class Place:
    def __init__(self):
        a, b = lax.axis_index("gx"), lax.axis_index("gy")
        self.core, self.x, self.zh, self.y, self.zl = a % 2, (a // 2) % 4, a // 8, b // 4, b % 4
        self.other = 1 - self.core
        self.edge = self.x == 3 * self.core
        self.partner = self.at(core=self.other)
        self.outer = ((a + 31 + 2 * self.core) % 32, b)
        self.down, self.up = (a, (b + 15) % 16), (a, (b + 1) % 16)
        self.source = self.at(x=3 * self.core)
        self.final = self.at(core=self.other, x=3 * self.other, zh=(self.zh + 3 + 2 * self.core) % 4)
        self.reached = [
            self.at(core=self.other, x=p, zh=(self.zh + 3 + 2 * self.core) % 4) for p in range(4)
        ]
        self.turn = [(self.x + k) % 4 for k in range(1, 4)]

    def at(self, core=None, x=None, zh=None, y=None, zl=None):
        core = self.core if core is None else core
        x = self.x if x is None else x
        zh = self.zh if zh is None else zh
        y = self.y if y is None else y
        zl = self.zl if zl is None else zl
        return ((zh * 4 + x) * 2 + core, y * 4 + zl)


def signal(peers):
    barrier = pltpu.get_barrier_semaphore()
    for peer in peers:
        pl.semaphore_signal(barrier, inc=1, device_id=peer, device_id_type=MESH)


def greet(here, peers):
    barrier = pltpu.get_barrier_semaphore()
    peers = [here.partner, here.down, here.up, *peers]
    signal(peers)

    @pl.when(here.edge)
    def _():
        signal([here.at(x=p) for p in here.turn] + here.reached)
        pl.semaphore_wait(barrier, len(peers) + 7)

    @pl.when(jnp.logical_not(here.edge))
    def _():
        signal([here.source, here.final, here.outer])
        pl.semaphore_wait(barrier, len(peers) + 3)


def quarter(ref, p):
    return ref.at[p // 2, pl.ds(p % 2 * 64, 64)]


def flat_wait(ref, sem):
    pltpu.make_async_copy(ref, ref, sem).wait()


EXCHANGE_SCRATCH = [
    pltpu.VMEM((64, 512), BF16),
    pltpu.SemaphoreType.DMA((4,)),
    pltpu.SemaphoreType.DMA((4,)),
    pltpu.SemaphoreType.DMA((4,)),
    pltpu.SemaphoreType.DMA((4,)),
    pltpu.SemaphoreType.DMA((2,)),
]


def exchange_start(here, src, dst, relay, s, r, sq, rq, hop):
    @pl.when(here.edge)
    def _():
        for p in here.turn:
            send(quarter(src[1], p), relay, sq.at[p], hop.at[0], here.at(x=p))
        send(quarter(src[1], here.x), quarter(dst[1], here.x), sq.at[here.x], rq.at[here.x], here.final)

    send(src[3], dst[2], s.at[3], r.at[2], here.up)
    send(src[2], dst[3], s.at[2], r.at[3], here.down)
    send(src[0], dst[0], s.at[0], r.at[0], here.partner)

    @pl.when(jnp.logical_not(here.edge))
    def _():
        send(src[1], dst[1], s.at[1], r.at[1], here.outer)


def exchange_relay(here, src, dst, relay, s, r, sq, rq, hop):
    @pl.when(jnp.logical_not(here.edge))
    def _():
        flat_wait(relay, hop.at[0])
        send(relay, quarter(dst[1], here.x), hop.at[1], rq.at[here.x], here.final)


def exchange_finish(here, src, dst, relay, s, r, sq, rq, hop):
    for d in (0, 2, 3):
        flat_wait(dst[d], r.at[d])

    @pl.when(here.edge)
    def _():
        for p in range(4):
            flat_wait(relay, rq.at[p])
        for p in range(4):
            flat_wait(relay, sq.at[p])

    @pl.when(jnp.logical_not(here.edge))
    def _():
        flat_wait(dst[1], r.at[1])
        flat_wait(src[1], s.at[1])
        flat_wait(relay, hop.at[1])

    for d in (0, 2, 3):
        flat_wait(src[d], s.at[d])


def side_of(code, even):
    swapped = jnp.where(code < 4, code + 2, code - 2)
    return jnp.where(even & (code >= 2) & (code < 6), swapped, code)


def layer_kernel(
    patch_count, point_count, neighbours, neighbour_points,
    feats, w_query_hbm, w_key_hbm, w_value_hbm, out_grad_hbm,
    mixed, feat_grad, summed,
    w_query, w_key, w_value, out_grad,
    table, rows, turned, keys, values, query, dquery, dkeys, dvalues,
    term, own_grad, far_grad, back,
    away, own, from0, half, from1, part1, from2, part2, from3, from4, whole,
    loads, s0, r0, s1, r1, s2, r2, s3, r3, s4, r4, s5, r5, s6, r6, s7, r7, s8, r8,
    *scratch,
):
    slots, points, width = feats.shape
    near = neighbours.shape[-1]
    entries = near + 1
    per = entries * points
    here = Place()
    core, x, y, zh, zl = here.core, here.x, here.y, here.zh, here.zl
    xs, ys, hs, ls = ([(i + k) % 4 for k in range(1, 4)] for i in (x, y, zh, zl))
    x_devices = [here.at(x=i) for i in xs]
    y_devices = [here.at(y=i) for i in ys]
    h_devices = [here.at(zh=i) for i in hs]
    l_devices = [here.at(zl=i) for i in ls]
    orders = ((x, xs, x_devices, y, ys, y_devices), (y, ys, y_devices, x, xs, x_devices))
    pieces = [(h, k) for k in range(3) for h in range(2)] + [(0, 3), (1, 3)]
    ahead, behind = scratch[: len(scratch) // 2], scratch[len(scratch) // 2 :]

    started = []
    for n, (src, dst) in enumerate(
        [
            (w_query_hbm, w_query),
            (w_key_hbm, w_key),
            (w_value_hbm, w_value),
            (out_grad_hbm, out_grad),
            (feats, table.at[pl.ds(0, slots)]),
        ]
    ):
        started.append(pltpu.make_async_copy(src, dst, loads.at[n]))
        started[-1].start()
    greet(here, [*x_devices, *y_devices, *h_devices, *l_devices])
    src = [feats] * 4
    dst = [table.at[pl.ds(2 + 2 * d, 2)] for d in range(4)]
    exchange_start(here, src, dst, *ahead)

    for copy in started:
        copy.wait()
    for s in range(slots):
        query[pl.ds(s * points, points), :] = dot(feats[s], w_query[...]).astype(BF16)
    for s in range(slots):
        part = pl.ds(s * per, points)
        rows[part, :] = feats[s]
        keys[part, :] = dot(feats[s], w_key[...]).astype(BF16)
        values[part, :] = dot(feats[s], w_value[...]).astype(BF16)
    exchange_relay(here, src, dst, *ahead)
    exchange_finish(here, src, dst, *ahead)

    even = core == 0
    places = []
    for s in range(slots):
        places.append([s] + [side_of(neighbours[0, 0, s, m], even) for m in range(near)])
        for m in range(1, entries):
            rows[pl.ds((s * entries + m) * points, points), :] = table[places[s][m]]
        part = pl.ds(s * per + points, near * points)
        keys[part, :] = dot(rows[part, :], w_key[...]).astype(BF16)
        values[part, :] = dot(rows[part, :], w_value[...]).astype(BF16)
        part = pl.ds(s * per, per)
        turned[:, part] = rows[part, :].T

    lane = lax.broadcasted_iota(jnp.int32, (points, 128), 1)
    row = lax.broadcasted_iota(jnp.int32, (points, 128), 0)
    low = lane < 64
    lives, biases = [], []
    for s in range(slots):
        count = jnp.where(s < patch_count[0, 0], point_count[0, 0, s], 0)
        lives.append(row < count)
        bias = []
        for m in range(entries):
            most = point_count[0, 0, s] if m == 0 else neighbour_points[0, 0, s, m - 1]
            bias.append(jnp.where((row >= most) & (lane == 0), -1e30, 0.0).astype(BF16))
        biases.append(jnp.concatenate(bias, axis=0))
    one = jnp.where(lax.broadcasted_iota(jnp.int32, (2 * points, 128), 1) == 0, 1.0, 0.0).astype(BF16)
    upper = lax.broadcasted_iota(jnp.int32, (128, points), 0) < 64

    def heads(s, pair):
        part = pl.ds(s * per, per)
        mine = pl.ds(s * points, points)
        lanes = pl.ds(pair * 128, 128)
        live = lives[s]
        kk = keys[part, lanes]
        vv = values[part, lanes]
        qq = query[mine, lanes].astype(F32) * 0.125
        gg = jnp.where(live, out_grad[s, :, lanes].astype(F32), 0.0)
        qq = jnp.concatenate([jnp.where(low, qq, 0.0), jnp.where(low, 0.0, qq)], axis=0).astype(BF16)
        gg = jnp.concatenate([jnp.where(low, gg, 0.0), jnp.where(low, 0.0, gg)], axis=0).astype(BF16)
        score = dot(jnp.concatenate([kk, biases[s]], axis=1), jnp.concatenate([qq, one], axis=1), NT)
        dprob = dot(vv, gg, NT)
        top = jnp.max(score, axis=0, keepdims=True)
        expo = jnp.exp(score - top)
        inverse = 1.0 / jnp.sum(expo, axis=0, keepdims=True)
        prob = expo * inverse
        inner = jnp.sum(prob * dprob, axis=0, keepdims=True)
        dscore = (prob * (dprob - inner)).astype(BF16)
        prob = prob.astype(BF16)
        out = dot(vv, prob, TN)
        dq = dot(kk, dscore, TN)
        out = jnp.where(upper, out[:, :points], out[:, points:]).T
        dq = jnp.where(upper, dq[:, :points], dq[:, points:]).T
        mixed[s, :, lanes] = jnp.where(live, out, 0.0).astype(BF16)
        dquery[mine, lanes] = (dq * 0.125).astype(BF16)
        dkeys[part, lanes] = dot(dscore, qq).astype(BF16)
        dvalues[part, lanes] = dot(prob, gg).astype(BF16)

    def gradients(c, which):
        lanes = pl.ds(c * 256, 256)
        side = pl.ds(pl.multiple_of(which * 256, 256), 256)
        of_query = None
        for s in range(slots):
            part = dot(turned[side, pl.ds(s * per, points)], dquery[pl.ds(s * points, points), lanes])
            of_query = part if of_query is None else of_query + part
        return of_query, dot(turned[side, :], dkeys[:, lanes]), dot(turned[side, :], dvalues[:, lanes])

    def row_of(h, k):
        return h * 128 + (orders[h][1][k] if k < 3 else orders[h][0]) * 32

    def chunk(c):
        for i, part in enumerate(gradients(c, here.other)):
            away[c, :, i * 256 : (i + 1) * 256] = part.astype(BF16)
        swaps = []
        for n, (h, k) in enumerate(pieces):
            at = pl.ds(row_of(h, k), 32)
            swaps.append(
                send(away.at[c, at], from0.at[c, at], s0.at[c, n], r0.at[c, n], here.partner)
            )
        for i, part in enumerate(gradients(c, core)):
            own[c, :, i * 256 : (i + 1) * 256] = part
        yield
        first = {}
        for n, (h, k) in enumerate(pieces):
            at = pl.ds(row_of(h, k), 32)
            swaps[n].wait_recv()
            half[c, at, :] = (own[c, at, :] + from0[c, at, :].astype(F32)).astype(BF16)
            if k < 3:
                first[h, k] = send(
                    half.at[c, at], from1.at[c, h, k], s1.at[c, h, k], r1.at[c, h, k], orders[h][2][k]
                )
        yield
        second = {}
        for h, (me, _, _, _, others, devices) in enumerate(orders):
            acc = half[c, pl.ds(h * 128 + me * 32, 32), :].astype(F32)
            for k in range(3):
                first[h, k].wait_recv()
                acc = acc + from1[c, h, k].astype(F32)
            part1[c, h] = acc.astype(BF16)
            for k in range(3):
                i = others[k]
                second[h, k] = send(
                    part1.at[c, h, pl.ds(i // 2 * 16, 16), pl.ds(i % 2 * 384, 384)],
                    from2.at[c, h, k],
                    s2.at[c, h, k],
                    r2.at[c, h, k],
                    devices[k],
                )
        part2[c, pl.ds(6, 2)] = jnp.zeros((2, 16, 128), BF16)
        yield
        for h, (_, _, _, me, _, _) in enumerate(orders):
            acc = part1[c, h, pl.ds(me // 2 * 16, 16), pl.ds(me % 2 * 384, 384)].astype(F32)
            for k in range(3):
                second[h, k].wait_recv()
                acc = acc + from2[c, h, k].astype(F32)
            acc = acc.astype(BF16)
            for t in range(3):
                part2[c, 3 * h + t] = acc[:, t * 128 : (t + 1) * 128]
        third = [
            send(part2.at[c, pl.ds(ls[k] * 2, 2)], from3.at[c, k], s3.at[c, k], r3.at[c, k], l_devices[k])
            for k in range(3)
        ]
        yield
        acc = part2[c, pl.ds(zl * 2, 2)].astype(F32)
        for k in range(3):
            third[k].wait_recv()
            acc = acc + from3[c, k].astype(F32)
        from4[c, zh] = acc.astype(BF16)
        fourth = [
            send(from4.at[c, zh], from4.at[c, zh], s4.at[c, k], r4.at[c, k], h_devices[k])
            for k in range(3)
        ]
        yield
        for k in range(3):
            fourth[k].wait_recv()
        acc = from4[c, 0].astype(F32)
        for i in range(1, 4):
            acc = acc + from4[c, i].astype(F32)
        mine = whole.at[c, pl.ds(zl * 2, 2)]
        mine[...] = acc.astype(BF16)
        fifth = [send(mine, mine, s5.at[c, k], r5.at[c, k], l_devices[k]) for k in range(3)]
        yield
        for k in range(3):
            fifth[k].wait_recv()
        sixth = {}
        for h, (me, _, _, place, _, devices) in enumerate(orders):
            mine = summed.at[
                c, pl.ds(core * 256 + h * 128 + me * 32 + place // 2 * 16, 16), pl.ds(place % 2 * 384, 384)
            ]
            mine[...] = jnp.concatenate([whole[c, 3 * h + t] for t in range(3)], axis=1)
            for k in range(3):
                sixth[h, k] = send(mine, mine, s6.at[c, h, k], r6.at[c, h, k], devices[k])
        yield
        seventh, eighth = {}, []
        for h, (me, _, devices, _, _, _) in enumerate(orders):
            for k in range(3):
                sixth[h, k].wait_recv()
            mine = summed.at[c, pl.ds(core * 256 + h * 128 + me * 32, 32)]
            for k in range(3):
                seventh[h, k] = send(mine, mine, s7.at[c, h, k], r7.at[c, h, k], devices[k])
            eighth.append(send(mine, mine, s8.at[c, h, 3], r8.at[c, h, 3], here.partner))
        yield
        for k in (0, 2, 1):
            for h, (me, _, _, _, _, _) in enumerate(orders):
                seventh[h, k].wait_recv()
                mine = summed.at[c, pl.ds(core * 256 + h * 128 + (me + 3 - k) % 4 * 32, 32)]
                eighth.append(send(mine, mine, s8.at[c, h, k], r8.at[c, h, k], here.partner))
        yield
        for copy in eighth:
            copy.wait()
        for copy in [
            *swaps, *first.values(), *second.values(), *third, *fourth, *fifth,
            *sixth.values(), *seventh.values(),
        ]:
            copy.wait_send()
        yield

    def terms():
        for s in range(slots):
            part = pl.ds(s * per, per)
            value = dot(dkeys[part, :], w_key[...], NT) + dot(dvalues[part, :], w_value[...], NT)
            term[pl.ds(s * entries, entries)] = value.reshape(entries, points, width)
        for t in range(5 * slots):
            acc = None
            for s in range(slots):
                number, at = 0, 0
                for m in reversed(range(entries)):
                    same = places[s][m] == t
                    number = number + jnp.where(same, 1, 0)
                    at = jnp.where(same, m, at)
                value = term[s * entries + at] * number.astype(F32)
                acc = value if acc is None else acc + value
            if t < slots:
                mine = dquery[pl.ds(t * points, points), :]
                own_grad[t] = acc + dot(mine, w_query[...], NT)
            else:
                far_grad[t - slots] = acc.astype(BF16)

    for pair in range(2):
        for s in range(slots):
            heads(s, pair)
    one_chunk, two_chunk = chunk(0), chunk(1)
    next(one_chunk)
    heads(0, 2)
    next(one_chunk)
    heads(1, 2)
    heads(0, 3)
    next(one_chunk)
    heads(1, 3)
    next(one_chunk)
    next(two_chunk)
    next(two_chunk)
    next(one_chunk)
    terms()
    next(two_chunk)
    next(two_chunk)
    next(one_chunk)
    next(two_chunk)
    next(one_chunk)
    next(two_chunk)
    src = [far_grad.at[pl.ds(2 * d, 2)] for d in range(4)]
    dst = [back.at[d] for d in range(4)]
    exchange_start(here, src, dst, *behind)
    next(one_chunk)
    next(two_chunk)
    exchange_relay(here, src, dst, *behind)
    next(one_chunk)
    next(two_chunk)
    next(two_chunk)
    exchange_finish(here, src, dst, *behind)
    acc = own_grad[...]
    for d in range(4):
        acc = acc + back[d].astype(F32)
    feat_grad[...] = acc.astype(BF16)
    next(one_chunk)
    next(two_chunk)


def layer(patch_count, point_count, neighbours, neighbour_points, feats, w_query, w_key, w_value, out_grad):
    slots, points, width = feats.shape
    entries = slots * (neighbours.shape[-1] + 1)
    own, every = slots * points, entries * points
    dma = pltpu.SemaphoreType.DMA
    smem = pl.BlockSpec(memory_space=pltpu.SMEM)
    vmem = pl.BlockSpec(memory_space=pltpu.VMEM)
    hbm = pl.BlockSpec(memory_space=pl.ANY)

    def held(*shape, kind=BF16):
        return pltpu.VMEM(shape, kind)

    return pl.pallas_call(
        layer_kernel,
        out_shape=[
            jax.ShapeDtypeStruct((slots, points, width), BF16),
            jax.ShapeDtypeStruct((slots, points, width), BF16),
            jax.ShapeDtypeStruct((2, 512, 768), BF16),
        ],
        in_specs=[smem] * 4 + [vmem] + [hbm] * 4,
        out_specs=[vmem] * 3,
        scratch_shapes=[
            held(width, width), held(width, width), held(width, width), held(slots, points, width),
            held(5 * slots, points, width),
            held(every, width),
            held(width, every),
            held(every, width), held(every, width),
            held(own, width), held(own, width),
            held(every, width), held(every, width),
            held(entries, points, width, kind=F32),
            held(slots, points, width, kind=F32),
            held(4 * slots, points, width),
            held(4, slots, points, width),
            held(2, 256, 768), held(2, 256, 768, kind=F32),
            held(2, 256, 768), held(2, 256, 768),
            held(2, 2, 3, 32, 768), held(2, 2, 32, 768),
            held(2, 2, 3, 16, 384), held(2, 8, 16, 128),
            held(2, 3, 2, 16, 128), held(2, 4, 2, 16, 128), held(2, 8, 16, 128),
            dma((5,)),
            dma((2, 8)), dma((2, 8)),
            dma((2, 2, 3)), dma((2, 2, 3)),
            dma((2, 2, 3)), dma((2, 2, 3)),
            dma((2, 3)), dma((2, 3)),
            dma((2, 3)), dma((2, 3)),
            dma((2, 3)), dma((2, 3)),
            dma((2, 2, 3)), dma((2, 2, 3)),
            dma((2, 2, 3)), dma((2, 2, 3)),
            dma((2, 2, 4)), dma((2, 2, 4)),
            *EXCHANGE_SCRATCH,
            *EXCHANGE_SCRATCH,
        ],
        compiler_params=pltpu.CompilerParams(
            collective_id=0, has_side_effects=True, vmem_limit_bytes=VMEM_LIMIT
        ),
        name="layer",
    )(patch_count, point_count, neighbours, neighbour_points, feats, w_query, w_key, w_value, out_grad)


def finish_kernel(mixed, feat_grad, summed, mixed_out, feat_grad_out, of_query, of_key, of_value, sems):
    pairs = [(mixed, mixed_out), (feat_grad, feat_grad_out)]
    for i, out in enumerate((of_query, of_key, of_value)):
        for c in range(2):
            pairs.append((summed.at[c, :, pl.ds(i * 256, 256)], out.at[:, pl.ds(c * 256, 256)]))
    copies = [pltpu.make_async_copy(src, dst, sems.at[n]) for n, (src, dst) in enumerate(pairs)]
    for copy in copies:
        copy.start()
    for copy in copies:
        copy.wait()


def finish(mixed, feat_grad, summed):
    hbm = pl.BlockSpec(memory_space=pl.ANY)
    width = mixed.shape[2]
    return pl.pallas_call(
        finish_kernel,
        out_shape=[jax.ShapeDtypeStruct(mixed.shape, BF16)] * 2
        + [jax.ShapeDtypeStruct((width, width), BF16)] * 3,
        in_specs=[hbm] * 3,
        out_specs=[hbm] * 5,
        scratch_shapes=[pltpu.SemaphoreType.DMA((8,))],
        name="finish",
    )(mixed, feat_grad, summed)


def body(
    feats, w_query, w_key, w_value, out_grad, patch_count, point_count, neighbours, neighbour_points
):
    slots, points, width = (feats.shape[2], feats.shape[3], feats.shape[4])
    mixed, feat_grad, summed = layer(
        patch_count, point_count, neighbours, neighbour_points,
        feats.reshape(slots, points, width), w_query, w_key, w_value,
        out_grad.reshape(slots, points, width),
    )
    mixed, feat_grad, *sums = finish(mixed, feat_grad, summed)
    return (mixed.reshape(feats.shape), feat_grad.reshape(feats.shape), *sums)


def solution(mesh):
    return jax.shard_map(
        body,
        mesh=mesh,
        in_specs=(
            P("gx", "gy", None, None, None),
            P(),
            P(),
            P(),
            P("gx", "gy", None, None, None),
            P("gx", "gy"),
            P("gx", "gy", None),
            P("gx", "gy", None, None),
            P("gx", "gy", None, None),
        ),
        out_specs=(P("gx", "gy", None, None, None), P("gx", "gy", None, None, None), P(), P(), P()),
        check_vma=False,
    )
```

```python
import functools

import jax
import jax.numpy as jnp
from jax import lax
from jax.experimental import pallas as pl
from jax.experimental.pallas import tpu as pltpu
from jax.sharding import PartitionSpec as P

HEADS = 8
MESH = pl.DeviceIdType.MESH
VMEM_LIMIT = 56 * 1024 * 1024
F32 = jnp.float32
BF16 = jnp.bfloat16

NT = (((1,), (1,)), ((), ()))
TN = (((0,), (0,)), ((), ()))


def dot(a, b, dims=(((1,), (0,)), ((), ()))):
    return lax.dot_general(a, b, dims, preferred_element_type=F32)


def send(src, dst, send_sem, recv_sem, peer):
    copy = pltpu.make_async_remote_copy(
        src_ref=src,
        dst_ref=dst,
        send_sem=send_sem,
        recv_sem=recv_sem,
        device_id=peer,
        device_id_type=MESH,
    )
    copy.start()
    return copy


class Place:
    def __init__(self):
        a, b = lax.axis_index("gx"), lax.axis_index("gy")
        self.core, self.x, self.zh, self.y, self.zl = a % 2, (a // 2) % 4, a // 8, b // 4, b % 4
        self.other = 1 - self.core
        self.edge = self.x == 3 * self.core
        self.partner = self.at(core=self.other)
        self.outer = ((a + 31 + 2 * self.core) % 32, b)
        self.down, self.up = (a, (b + 15) % 16), (a, (b + 1) % 16)
        self.source = self.at(x=3 * self.core)
        self.final = self.at(core=self.other, x=3 * self.other, zh=(self.zh + 3 + 2 * self.core) % 4)
        self.reached = [
            self.at(core=self.other, x=p, zh=(self.zh + 3 + 2 * self.core) % 4) for p in range(4)
        ]
        self.turn = [(self.x + k) % 4 for k in range(1, 4)]

    def at(self, core=None, x=None, zh=None, y=None, zl=None):
        core = self.core if core is None else core
        x = self.x if x is None else x
        zh = self.zh if zh is None else zh
        y = self.y if y is None else y
        zl = self.zl if zl is None else zl
        return ((zh * 4 + x) * 2 + core, y * 4 + zl)


def signal(peers):
    barrier = pltpu.get_barrier_semaphore()
    for peer in peers:
        pl.semaphore_signal(barrier, inc=1, device_id=peer, device_id_type=MESH)


def greet(here, peers):
    barrier = pltpu.get_barrier_semaphore()
    peers = [here.partner, here.down, here.up, *peers]
    signal(peers)

    @pl.when(here.edge)
    def _():
        signal([here.at(x=p) for p in here.turn] + here.reached)
        pl.semaphore_wait(barrier, len(peers) + 7)

    @pl.when(jnp.logical_not(here.edge))
    def _():
        signal([here.source, here.final, here.outer])
        pl.semaphore_wait(barrier, len(peers) + 3)


def quarter(ref, p):
    return ref.at[p // 2, pl.ds(p % 2 * 64, 64)]


def flat_wait(ref, sem):
    pltpu.make_async_copy(ref, ref, sem).wait()


EXCHANGE_SCRATCH = [
    pltpu.VMEM((64, 512), BF16),
    pltpu.SemaphoreType.DMA((4,)),
    pltpu.SemaphoreType.DMA((4,)),
    pltpu.SemaphoreType.DMA((4,)),
    pltpu.SemaphoreType.DMA((4,)),
    pltpu.SemaphoreType.DMA((2,)),
]


def exchange_start(here, src, dst, relay, s, r, sq, rq, hop):
    @pl.when(here.edge)
    def _():
        for p in here.turn:
            send(quarter(src[1], p), relay, sq.at[p], hop.at[0], here.at(x=p))
        send(quarter(src[1], here.x), quarter(dst[1], here.x), sq.at[here.x], rq.at[here.x], here.final)

    send(src[3], dst[2], s.at[3], r.at[2], here.up)
    send(src[2], dst[3], s.at[2], r.at[3], here.down)
    send(src[0], dst[0], s.at[0], r.at[0], here.partner)

    @pl.when(jnp.logical_not(here.edge))
    def _():
        send(src[1], dst[1], s.at[1], r.at[1], here.outer)


def exchange_relay(here, src, dst, relay, s, r, sq, rq, hop):
    @pl.when(jnp.logical_not(here.edge))
    def _():
        flat_wait(relay, hop.at[0])
        send(relay, quarter(dst[1], here.x), hop.at[1], rq.at[here.x], here.final)


def exchange_finish(here, src, dst, relay, s, r, sq, rq, hop):
    for d in (0, 2, 3):
        flat_wait(dst[d], r.at[d])

    @pl.when(here.edge)
    def _():
        for p in range(4):
            flat_wait(relay, rq.at[p])
        for p in range(4):
            flat_wait(relay, sq.at[p])

    @pl.when(jnp.logical_not(here.edge))
    def _():
        flat_wait(dst[1], r.at[1])
        flat_wait(src[1], s.at[1])
        flat_wait(relay, hop.at[1])

    for d in (0, 2, 3):
        flat_wait(src[d], s.at[d])


def side_of(code, even):
    swapped = jnp.where(code < 4, code + 2, code - 2)
    return jnp.where(even & (code >= 2) & (code < 6), swapped, code)


def layer_kernel(
    patch_count, point_count, neighbours, neighbour_points,
    feats, w_query_hbm, w_key_hbm, w_value_hbm, out_grad_hbm,
    mixed, feat_grad, summed,
    w_query, w_key, w_value, out_grad,
    table, rows, turned, keys, values, query, dquery, dkeys, dvalues,
    term, own_grad, far_grad, back,
    away, own, from0, half, from1, part1, from2, part2, from3, from4, whole,
    loads, s0, r0, s1, r1, s2, r2, s3, r3, s4, r4, s5, r5, s6, r6, s7, r7, s8, r8,
    *scratch,
):
    slots, points, width = feats.shape
    near = neighbours.shape[-1]
    entries = near + 1
    per = entries * points
    here = Place()
    core, x, y, zh, zl = here.core, here.x, here.y, here.zh, here.zl
    xs, ys, hs, ls = ([(i + k) % 4 for k in range(1, 4)] for i in (x, y, zh, zl))
    x_devices = [here.at(x=i) for i in xs]
    y_devices = [here.at(y=i) for i in ys]
    h_devices = [here.at(zh=i) for i in hs]
    l_devices = [here.at(zl=i) for i in ls]
    orders = ((x, xs, x_devices, y, ys, y_devices), (y, ys, y_devices, x, xs, x_devices))
    pieces = [(h, k) for k in range(3) for h in range(2)] + [(0, 3), (1, 3)]
    ahead, behind = scratch[: len(scratch) // 2], scratch[len(scratch) // 2 :]

    started = []
    for n, (src, dst) in enumerate(
        [
            (w_query_hbm, w_query),
            (w_key_hbm, w_key),
            (w_value_hbm, w_value),
            (out_grad_hbm, out_grad),
            (feats, table.at[pl.ds(0, slots)]),
        ]
    ):
        started.append(pltpu.make_async_copy(src, dst, loads.at[n]))
        started[-1].start()
    greet(here, [*x_devices, *y_devices, *h_devices, *l_devices])
    src = [feats] * 4
    dst = [table.at[pl.ds(2 + 2 * d, 2)] for d in range(4)]
    exchange_start(here, src, dst, *ahead)

    for copy in started:
        copy.wait()
    for s in range(slots):
        query[pl.ds(s * points, points), :] = dot(feats[s], w_query[...]).astype(BF16)
    for s in range(slots):
        part = pl.ds(s * per, points)
        rows[part, :] = feats[s]
        keys[part, :] = dot(feats[s], w_key[...]).astype(BF16)
        values[part, :] = dot(feats[s], w_value[...]).astype(BF16)
    exchange_relay(here, src, dst, *ahead)
    exchange_finish(here, src, dst, *ahead)

    even = core == 0
    places = []
    for s in range(slots):
        places.append([s] + [side_of(neighbours[0, 0, s, m], even) for m in range(near)])
        for m in range(1, entries):
            rows[pl.ds((s * entries + m) * points, points), :] = table[places[s][m]]
        part = pl.ds(s * per + points, near * points)
        keys[part, :] = dot(rows[part, :], w_key[...]).astype(BF16)
        values[part, :] = dot(rows[part, :], w_value[...]).astype(BF16)
        part = pl.ds(s * per, per)
        turned[:, part] = rows[part, :].T

    lane = lax.broadcasted_iota(jnp.int32, (points, 128), 1)
    row = lax.broadcasted_iota(jnp.int32, (points, 128), 0)
    low = lane < 64
    lives, biases = [], []
    for s in range(slots):
        count = jnp.where(s < patch_count[0, 0], point_count[0, 0, s], 0)
        lives.append(row < count)
        bias = []
        for m in range(entries):
            most = point_count[0, 0, s] if m == 0 else neighbour_points[0, 0, s, m - 1]
            bias.append(jnp.where((row >= most) & (lane == 0), -1e30, 0.0).astype(BF16))
        biases.append(jnp.concatenate(bias, axis=0))
    one = jnp.where(lax.broadcasted_iota(jnp.int32, (2 * points, 128), 1) == 0, 1.0, 0.0).astype(BF16)
    upper = lax.broadcasted_iota(jnp.int32, (128, points), 0) < 64

    def heads(s, pair):
        part = pl.ds(s * per, per)
        mine = pl.ds(s * points, points)
        lanes = pl.ds(pair * 128, 128)
        live = lives[s]
        kk = keys[part, lanes]
        vv = values[part, lanes]
        qq = query[mine, lanes].astype(F32) * 0.125
        gg = jnp.where(live, out_grad[s, :, lanes].astype(F32), 0.0)
        qq = jnp.concatenate([jnp.where(low, qq, 0.0), jnp.where(low, 0.0, qq)], axis=0).astype(BF16)
        gg = jnp.concatenate([jnp.where(low, gg, 0.0), jnp.where(low, 0.0, gg)], axis=0).astype(BF16)
        score = dot(jnp.concatenate([kk, biases[s]], axis=1), jnp.concatenate([qq, one], axis=1), NT)
        dprob = dot(vv, gg, NT)
        top = jnp.max(score, axis=0, keepdims=True)
        expo = jnp.exp(score - top)
        inverse = 1.0 / jnp.sum(expo, axis=0, keepdims=True)
        prob = expo * inverse
        inner = jnp.sum(prob * dprob, axis=0, keepdims=True)
        dscore = (prob * (dprob - inner)).astype(BF16)
        prob = prob.astype(BF16)
        out = dot(vv, prob, TN)
        dq = dot(kk, dscore, TN)
        out = jnp.where(upper, out[:, :points], out[:, points:]).T
        dq = jnp.where(upper, dq[:, :points], dq[:, points:]).T
        mixed[s, :, lanes] = jnp.where(live, out, 0.0).astype(BF16)
        dquery[mine, lanes] = (dq * 0.125).astype(BF16)
        dkeys[part, lanes] = dot(dscore, qq).astype(BF16)
        dvalues[part, lanes] = dot(prob, gg).astype(BF16)

    def gradients(c, which):
        lanes = pl.ds(c * 256, 256)
        side = pl.ds(pl.multiple_of(which * 256, 256), 256)
        of_query = None
        for s in range(slots):
            part = dot(turned[side, pl.ds(s * per, points)], dquery[pl.ds(s * points, points), lanes])
            of_query = part if of_query is None else of_query + part
        return of_query, dot(turned[side, :], dkeys[:, lanes]), dot(turned[side, :], dvalues[:, lanes])

    def row_of(h, k):
        return h * 128 + (orders[h][1][k] if k < 3 else orders[h][0]) * 32

    def chunk(c):
        for i, part in enumerate(gradients(c, here.other)):
            away[c, :, i * 256 : (i + 1) * 256] = part.astype(BF16)
        swaps = []
        for n, (h, k) in enumerate(pieces):
            at = pl.ds(row_of(h, k), 32)
            swaps.append(
                send(away.at[c, at], from0.at[c, at], s0.at[c, n], r0.at[c, n], here.partner)
            )
        for i, part in enumerate(gradients(c, core)):
            own[c, :, i * 256 : (i + 1) * 256] = part
        yield
        first = {}
        for n, (h, k) in enumerate(pieces):
            at = pl.ds(row_of(h, k), 32)
            swaps[n].wait_recv()
            half[c, at, :] = (own[c, at, :] + from0[c, at, :].astype(F32)).astype(BF16)
            if k < 3:
                first[h, k] = send(
                    half.at[c, at], from1.at[c, h, k], s1.at[c, h, k], r1.at[c, h, k], orders[h][2][k]
                )
        yield
        second = {}
        for h, (me, _, _, _, others, devices) in enumerate(orders):
            acc = half[c, pl.ds(h * 128 + me * 32, 32), :].astype(F32)
            for k in range(3):
                first[h, k].wait_recv()
                acc = acc + from1[c, h, k].astype(F32)
            part1[c, h] = acc.astype(BF16)
            for k in range(3):
                i = others[k]
                second[h, k] = send(
                    part1.at[c, h, pl.ds(i // 2 * 16, 16), pl.ds(i % 2 * 384, 384)],
                    from2.at[c, h, k],
                    s2.at[c, h, k],
                    r2.at[c, h, k],
                    devices[k],
                )
        part2[c, pl.ds(6, 2)] = jnp.zeros((2, 16, 128), BF16)
        yield
        for h, (_, _, _, me, _, _) in enumerate(orders):
            acc = part1[c, h, pl.ds(me // 2 * 16, 16), pl.ds(me % 2 * 384, 384)].astype(F32)
            for k in range(3):
                second[h, k].wait_recv()
                acc = acc + from2[c, h, k].astype(F32)
            acc = acc.astype(BF16)
            for t in range(3):
                part2[c, 3 * h + t] = acc[:, t * 128 : (t + 1) * 128]
        third = [
            send(part2.at[c, pl.ds(ls[k] * 2, 2)], from3.at[c, k], s3.at[c, k], r3.at[c, k], l_devices[k])
            for k in range(3)
        ]
        yield
        acc = part2[c, pl.ds(zl * 2, 2)].astype(F32)
        for k in range(3):
            third[k].wait_recv()
            acc = acc + from3[c, k].astype(F32)
        from4[c, zh] = acc.astype(BF16)
        fourth = [
            send(from4.at[c, zh], from4.at[c, zh], s4.at[c, k], r4.at[c, k], h_devices[k])
            for k in range(3)
        ]
        yield
        for k in range(3):
            fourth[k].wait_recv()
        acc = from4[c, 0].astype(F32)
        for i in range(1, 4):
            acc = acc + from4[c, i].astype(F32)
        mine = whole.at[c, pl.ds(zl * 2, 2)]
        mine[...] = acc.astype(BF16)
        fifth = [send(mine, mine, s5.at[c, k], r5.at[c, k], l_devices[k]) for k in range(3)]
        yield
        for k in range(3):
            fifth[k].wait_recv()
        sixth = {}
        for h, (me, _, _, place, _, devices) in enumerate(orders):
            mine = summed.at[
                c, pl.ds(core * 256 + h * 128 + me * 32 + place // 2 * 16, 16), pl.ds(place % 2 * 384, 384)
            ]
            mine[...] = jnp.concatenate([whole[c, 3 * h + t] for t in range(3)], axis=1)
            for k in range(3):
                sixth[h, k] = send(mine, mine, s6.at[c, h, k], r6.at[c, h, k], devices[k])
        yield
        seventh, eighth = {}, []
        for h, (me, _, devices, _, _, _) in enumerate(orders):
            for k in range(3):
                sixth[h, k].wait_recv()
            mine = summed.at[c, pl.ds(core * 256 + h * 128 + me * 32, 32)]
            for k in range(3):
                seventh[h, k] = send(mine, mine, s7.at[c, h, k], r7.at[c, h, k], devices[k])
            eighth.append(send(mine, mine, s8.at[c, h, 3], r8.at[c, h, 3], here.partner))
        yield
        for k in (0, 2, 1):
            for h, (me, _, _, _, _, _) in enumerate(orders):
                seventh[h, k].wait_recv()
                mine = summed.at[c, pl.ds(core * 256 + h * 128 + (me + 3 - k) % 4 * 32, 32)]
                eighth.append(send(mine, mine, s8.at[c, h, k], r8.at[c, h, k], here.partner))
        yield
        for copy in eighth:
            copy.wait()
        for copy in [
            *swaps, *first.values(), *second.values(), *third, *fourth, *fifth,
            *sixth.values(), *seventh.values(),
        ]:
            copy.wait_send()
        yield

    def terms():
        for s in range(slots):
            part = pl.ds(s * per, per)
            value = dot(dkeys[part, :], w_key[...], NT) + dot(dvalues[part, :], w_value[...], NT)
            term[pl.ds(s * entries, entries)] = value.reshape(entries, points, width)
        for t in range(5 * slots):
            acc = None
            for s in range(slots):
                number, at = 0, 0
                for m in reversed(range(entries)):
                    same = places[s][m] == t
                    number = number + jnp.where(same, 1, 0)
                    at = jnp.where(same, m, at)
                value = term[s * entries + at] * number.astype(F32)
                acc = value if acc is None else acc + value
            if t < slots:
                mine = dquery[pl.ds(t * points, points), :]
                own_grad[t] = acc + dot(mine, w_query[...], NT)
            else:
                far_grad[t - slots] = acc.astype(BF16)

    for pair in range(2):
        for s in range(slots):
            heads(s, pair)
    one_chunk, two_chunk = chunk(0), chunk(1)
    next(one_chunk)
    heads(0, 2)
    next(one_chunk)
    heads(1, 2)
    heads(0, 3)
    next(one_chunk)
    heads(1, 3)
    next(one_chunk)
    next(two_chunk)
    next(two_chunk)
    next(one_chunk)
    terms()
    next(two_chunk)
    next(two_chunk)
    next(one_chunk)
    next(two_chunk)
    next(one_chunk)
    next(two_chunk)
    src = [far_grad.at[pl.ds(2 * d, 2)] for d in range(4)]
    dst = [back.at[d] for d in range(4)]
    exchange_start(here, src, dst, *behind)
    next(one_chunk)
    next(two_chunk)
    exchange_relay(here, src, dst, *behind)
    next(one_chunk)
    next(two_chunk)
    next(two_chunk)
    exchange_finish(here, src, dst, *behind)
    acc = own_grad[...]
    for d in range(4):
        acc = acc + back[d].astype(F32)
    feat_grad[...] = acc.astype(BF16)
    next(one_chunk)
    next(two_chunk)


def layer(patch_count, point_count, neighbours, neighbour_points, feats, w_query, w_key, w_value, out_grad):
    slots, points, width = feats.shape
    entries = slots * (neighbours.shape[-1] + 1)
    own, every = slots * points, entries * points
    dma = pltpu.SemaphoreType.DMA
    smem = pl.BlockSpec(memory_space=pltpu.SMEM)
    vmem = pl.BlockSpec(memory_space=pltpu.VMEM)
    hbm = pl.BlockSpec(memory_space=pl.ANY)

    def held(*shape, kind=BF16):
        return pltpu.VMEM(shape, kind)

    return pl.pallas_call(
        layer_kernel,
        out_shape=[
            jax.ShapeDtypeStruct((slots, points, width), BF16),
            jax.ShapeDtypeStruct((slots, points, width), BF16),
            jax.ShapeDtypeStruct((2, 512, 768), BF16),
        ],
        in_specs=[smem] * 4 + [vmem] + [hbm] * 4,
        out_specs=[vmem] * 3,
        scratch_shapes=[
            held(width, width), held(width, width), held(width, width), held(slots, points, width),
            held(5 * slots, points, width),
            held(every, width),
            held(width, every),
            held(every, width), held(every, width),
            held(own, width), held(own, width),
            held(every, width), held(every, width),
            held(entries, points, width, kind=F32),
            held(slots, points, width, kind=F32),
            held(4 * slots, points, width),
            held(4, slots, points, width),
            held(2, 256, 768), held(2, 256, 768, kind=F32),
            held(2, 256, 768), held(2, 256, 768),
            held(2, 2, 3, 32, 768), held(2, 2, 32, 768),
            held(2, 2, 3, 16, 384), held(2, 8, 16, 128),
            held(2, 3, 2, 16, 128), held(2, 4, 2, 16, 128), held(2, 8, 16, 128),
            dma((5,)),
            dma((2, 8)), dma((2, 8)),
            dma((2, 2, 3)), dma((2, 2, 3)),
            dma((2, 2, 3)), dma((2, 2, 3)),
            dma((2, 3)), dma((2, 3)),
            dma((2, 3)), dma((2, 3)),
            dma((2, 3)), dma((2, 3)),
            dma((2, 2, 3)), dma((2, 2, 3)),
            dma((2, 2, 3)), dma((2, 2, 3)),
            dma((2, 2, 4)), dma((2, 2, 4)),
            *EXCHANGE_SCRATCH,
            *EXCHANGE_SCRATCH,
        ],
        compiler_params=pltpu.CompilerParams(
            collective_id=0, has_side_effects=True, vmem_limit_bytes=VMEM_LIMIT
        ),
        name="layer",
    )(patch_count, point_count, neighbours, neighbour_points, feats, w_query, w_key, w_value, out_grad)


def finish_kernel(mixed, feat_grad, summed, *rest):
    outs, (rows, sums, arrive, leave) = rest[:5], rest[5:]
    groups = [[(summed.at[c, :, pl.ds(i * 256, 256)], sums.at[i, :, pl.ds(c * 256, 256)]) for c in range(2)] for i in range(3)]
    groups += [[(mixed, rows.at[0])], [(feat_grad, rows.at[1])]]
    held = [sums.at[0], sums.at[1], sums.at[2], rows.at[0], rows.at[1]]
    outs = [*outs[2:], *outs[:2]]
    loads, n = [], 0
    for group in groups:
        loads.append([])
        for src, dst in group:
            loads[-1].append(pltpu.make_async_copy(src, dst, arrive.at[n]))
            loads[-1][-1].start()
            n += 1
    stores = []
    for i, group in enumerate(loads):
        for copy in group:
            copy.wait()
        stores.append(pltpu.make_async_copy(held[i], outs[i], leave.at[i]))
        stores[-1].start()
    for copy in stores:
        copy.wait()


def finish(mixed, feat_grad, summed):
    hbm = pl.BlockSpec(memory_space=pl.ANY)
    width = mixed.shape[2]
    return pl.pallas_call(
        finish_kernel,
        out_shape=[jax.ShapeDtypeStruct(mixed.shape, BF16)] * 2
        + [jax.ShapeDtypeStruct((width, width), BF16)] * 3,
        in_specs=[hbm] * 3,
        out_specs=[hbm] * 5,
        scratch_shapes=[
            pltpu.VMEM((2, *mixed.shape), BF16),
            pltpu.VMEM((3, width, width), BF16),
            pltpu.SemaphoreType.DMA((8,)),
            pltpu.SemaphoreType.DMA((5,)),
        ],
        compiler_params=pltpu.CompilerParams(vmem_limit_bytes=VMEM_LIMIT),
        name="finish",
    )(mixed, feat_grad, summed)


def body(
    feats, w_query, w_key, w_value, out_grad, patch_count, point_count, neighbours, neighbour_points
):
    slots, points, width = (feats.shape[2], feats.shape[3], feats.shape[4])
    mixed, feat_grad, summed = layer(
        patch_count, point_count, neighbours, neighbour_points,
        feats.reshape(slots, points, width), w_query, w_key, w_value,
        out_grad.reshape(slots, points, width),
    )
    mixed, feat_grad, *sums = finish(mixed, feat_grad, summed)
    return (mixed.reshape(feats.shape), feat_grad.reshape(feats.shape), *sums)


def solution(mesh):
    return jax.shard_map(
        body,
        mesh=mesh,
        in_specs=(
            P("gx", "gy", None, None, None),
            P(),
            P(),
            P(),
            P("gx", "gy", None, None, None),
            P("gx", "gy"),
            P("gx", "gy", None),
            P("gx", "gy", None, None),
            P("gx", "gy", None, None),
        ),
        out_specs=(P("gx", "gy", None, None, None), P("gx", "gy", None, None, None), P(), P(), P()),
        check_vma=False,
    )
```

```python
import functools

import jax
import jax.numpy as jnp
from jax import lax
from jax.experimental import pallas as pl
from jax.experimental.pallas import tpu as pltpu
from jax.sharding import PartitionSpec as P

HEADS = 8
MESH = pl.DeviceIdType.MESH
VMEM_LIMIT = 56 * 1024 * 1024
F32 = jnp.float32
BF16 = jnp.bfloat16

NT = (((1,), (1,)), ((), ()))
TN = (((0,), (0,)), ((), ()))


def dot(a, b, dims=(((1,), (0,)), ((), ()))):
    return lax.dot_general(a, b, dims, preferred_element_type=F32)


def send(src, dst, send_sem, recv_sem, peer):
    copy = pltpu.make_async_remote_copy(
        src_ref=src,
        dst_ref=dst,
        send_sem=send_sem,
        recv_sem=recv_sem,
        device_id=peer,
        device_id_type=MESH,
    )
    copy.start()
    return copy


class Place:
    def __init__(self):
        a, b = lax.axis_index("gx"), lax.axis_index("gy")
        self.core, self.x, self.zh, self.y, self.zl = a % 2, (a // 2) % 4, a // 8, b // 4, b % 4
        self.other = 1 - self.core
        self.edge = self.x == 3 * self.core
        self.partner = self.at(core=self.other)
        self.outer = ((a + 31 + 2 * self.core) % 32, b)
        self.down, self.up = (a, (b + 15) % 16), (a, (b + 1) % 16)
        self.source = self.at(x=3 * self.core)
        self.final = self.at(core=self.other, x=3 * self.other, zh=(self.zh + 3 + 2 * self.core) % 4)
        self.reached = [
            self.at(core=self.other, x=p, zh=(self.zh + 3 + 2 * self.core) % 4) for p in range(4)
        ]
        self.turn = [(self.x + k) % 4 for k in range(1, 4)]

    def at(self, core=None, x=None, zh=None, y=None, zl=None):
        core = self.core if core is None else core
        x = self.x if x is None else x
        zh = self.zh if zh is None else zh
        y = self.y if y is None else y
        zl = self.zl if zl is None else zl
        return ((zh * 4 + x) * 2 + core, y * 4 + zl)


def signal(peers):
    barrier = pltpu.get_barrier_semaphore()
    for peer in peers:
        pl.semaphore_signal(barrier, inc=1, device_id=peer, device_id_type=MESH)


def greet(here, peers):
    barrier = pltpu.get_barrier_semaphore()
    peers = [here.partner, here.down, here.up, *peers]
    signal(peers)

    @pl.when(here.edge)
    def _():
        signal([here.at(x=p) for p in here.turn] + here.reached)
        pl.semaphore_wait(barrier, len(peers) + 7)

    @pl.when(jnp.logical_not(here.edge))
    def _():
        signal([here.source, here.final, here.outer])
        pl.semaphore_wait(barrier, len(peers) + 3)


def quarter(ref, p):
    return ref.at[p // 2, pl.ds(p % 2 * 64, 64)]


def flat_wait(ref, sem):
    pltpu.make_async_copy(ref, ref, sem).wait()


EXCHANGE_SCRATCH = [
    pltpu.VMEM((64, 512), BF16),
    pltpu.SemaphoreType.DMA((4,)),
    pltpu.SemaphoreType.DMA((4,)),
    pltpu.SemaphoreType.DMA((4,)),
    pltpu.SemaphoreType.DMA((4,)),
    pltpu.SemaphoreType.DMA((2,)),
]


def exchange_start(here, src, dst, relay, s, r, sq, rq, hop):
    @pl.when(here.edge)
    def _():
        for p in here.turn:
            send(quarter(src[1], p), relay, sq.at[p], hop.at[0], here.at(x=p))
        send(quarter(src[1], here.x), quarter(dst[1], here.x), sq.at[here.x], rq.at[here.x], here.final)

    send(src[3], dst[2], s.at[3], r.at[2], here.up)
    send(src[2], dst[3], s.at[2], r.at[3], here.down)
    send(src[0], dst[0], s.at[0], r.at[0], here.partner)

    @pl.when(jnp.logical_not(here.edge))
    def _():
        send(src[1], dst[1], s.at[1], r.at[1], here.outer)


def exchange_relay(here, src, dst, relay, s, r, sq, rq, hop):
    @pl.when(jnp.logical_not(here.edge))
    def _():
        flat_wait(relay, hop.at[0])
        send(relay, quarter(dst[1], here.x), hop.at[1], rq.at[here.x], here.final)


def exchange_finish(here, src, dst, relay, s, r, sq, rq, hop):
    for d in (0, 2, 3):
        flat_wait(dst[d], r.at[d])

    @pl.when(here.edge)
    def _():
        for p in range(4):
            flat_wait(relay, rq.at[p])
        for p in range(4):
            flat_wait(relay, sq.at[p])

    @pl.when(jnp.logical_not(here.edge))
    def _():
        flat_wait(dst[1], r.at[1])
        flat_wait(src[1], s.at[1])
        flat_wait(relay, hop.at[1])

    for d in (0, 2, 3):
        flat_wait(src[d], s.at[d])


def side_of(code, even):
    swapped = jnp.where(code < 4, code + 2, code - 2)
    return jnp.where(even & (code >= 2) & (code < 6), swapped, code)


RETURN_AT = 3


def layer_kernel(
    patch_count, point_count, neighbours, neighbour_points,
    feats, w_query_hbm, w_key_hbm, w_value_hbm, out_grad_hbm,
    mixed, feat_grad, summed,
    w_query, w_key, w_value, out_grad,
    table, rows, turned, keys, values, query, dquery, dkeys, dvalues,
    term, own_grad, far_grad, back,
    away, own, from0, half, from1, part1, from2, tiles,
    loads, s0, r0, s1, r1, s2, r2, s3, r3, s4, r4, s5, r5, s6, r6,
    *scratch,
):
    slots, points, width = feats.shape
    near = neighbours.shape[-1]
    entries = near + 1
    per = entries * points
    here = Place()
    core, x, y, zh, zl = here.core, here.x, here.y, here.zh, here.zl
    axes = (("zl", "x", "y"), ("x", "y", "zl"), ("y", "x", "zl"))
    place = {"x": x, "y": y, "zl": zl, "zh": zh}

    def moved(**steps):
        return here.at(**{axis: (place[axis] + by) % 4 for axis, by in steps.items()})

    lines = [[moved(**{line: k}) for k in range(1, 4)] for line, _, _ in axes]
    steps = sorted(((i, j) for i in range(4) for j in range(4) if i + j), key=lambda t: -min(t[0], 4 - t[0]) - t[1])
    planes = [[moved(**{u: i, v: j}) for i, j in steps] for _, u, v in axes]
    deep = [moved(zh=k) for k in range(1, 4)]
    pieces = [(p, k) for k in range(4) for p in range(3)]
    ahead, behind = scratch[: len(scratch) // 2], scratch[len(scratch) // 2 :]

    started = []
    for n, (src, dst) in enumerate(
        [
            (w_query_hbm, w_query),
            (w_key_hbm, w_key),
            (w_value_hbm, w_value),
            (out_grad_hbm, out_grad),
            (feats, table.at[pl.ds(0, slots)]),
        ]
    ):
        started.append(pltpu.make_async_copy(src, dst, loads.at[n]))
        started[-1].start()
    crosswise = [
        moved(**{u: i, v: j}) for u, v in (("x", "y"), ("x", "zl"), ("y", "zl"))
        for i in range(1, 4) for j in range(1, 4)
    ]
    greet(here, [*lines[0], *lines[1], *lines[2], *deep, *crosswise])
    src = [feats] * 4
    dst = [table.at[pl.ds(2 + 2 * d, 2)] for d in range(4)]
    exchange_start(here, src, dst, *ahead)

    for copy in started:
        copy.wait()
    for s in range(slots):
        query[pl.ds(s * points, points), :] = dot(feats[s], w_query[...]).astype(BF16)
    for s in range(slots):
        part = pl.ds(s * per, points)
        rows[part, :] = feats[s]
        keys[part, :] = dot(feats[s], w_key[...]).astype(BF16)
        values[part, :] = dot(feats[s], w_value[...]).astype(BF16)
    exchange_relay(here, src, dst, *ahead)
    exchange_finish(here, src, dst, *ahead)

    even = core == 0
    places = []
    for s in range(slots):
        places.append([s] + [side_of(neighbours[0, 0, s, m], even) for m in range(near)])
        for m in range(1, entries):
            rows[pl.ds((s * entries + m) * points, points), :] = table[places[s][m]]
        part = pl.ds(s * per + points, near * points)
        keys[part, :] = dot(rows[part, :], w_key[...]).astype(BF16)
        values[part, :] = dot(rows[part, :], w_value[...]).astype(BF16)
        part = pl.ds(s * per, per)
        turned[:, part] = rows[part, :].T

    lane = lax.broadcasted_iota(jnp.int32, (points, 128), 1)
    row = lax.broadcasted_iota(jnp.int32, (points, 128), 0)
    low = lane < 64
    lives, biases = [], []
    for s in range(slots):
        count = jnp.where(s < patch_count[0, 0], point_count[0, 0, s], 0)
        lives.append(row < count)
        bias = []
        for m in range(entries):
            most = point_count[0, 0, s] if m == 0 else neighbour_points[0, 0, s, m - 1]
            bias.append(jnp.where((row >= most) & (lane == 0), -1e30, 0.0).astype(BF16))
        biases.append(jnp.concatenate(bias, axis=0))
    one = jnp.where(lax.broadcasted_iota(jnp.int32, (2 * points, 128), 1) == 0, 1.0, 0.0).astype(BF16)
    upper = lax.broadcasted_iota(jnp.int32, (128, points), 0) < 64

    def heads(s, pair):
        part = pl.ds(s * per, per)
        mine = pl.ds(s * points, points)
        lanes = pl.ds(pair * 128, 128)
        live = lives[s]
        kk = keys[part, lanes]
        vv = values[part, lanes]
        qq = query[mine, lanes].astype(F32) * 0.125
        gg = jnp.where(live, out_grad[s, :, lanes].astype(F32), 0.0)
        qq = jnp.concatenate([jnp.where(low, qq, 0.0), jnp.where(low, 0.0, qq)], axis=0).astype(BF16)
        gg = jnp.concatenate([jnp.where(low, gg, 0.0), jnp.where(low, 0.0, gg)], axis=0).astype(BF16)
        score = dot(jnp.concatenate([kk, biases[s]], axis=1), jnp.concatenate([qq, one], axis=1), NT)
        dprob = dot(vv, gg, NT)
        top = jnp.max(score, axis=0, keepdims=True)
        expo = jnp.exp(score - top)
        inverse = 1.0 / jnp.sum(expo, axis=0, keepdims=True)
        prob = expo * inverse
        inner = jnp.sum(prob * dprob, axis=0, keepdims=True)
        dscore = (prob * (dprob - inner)).astype(BF16)
        prob = prob.astype(BF16)
        out = dot(vv, prob, TN)
        dq = dot(kk, dscore, TN)
        out = jnp.where(upper, out[:, :points], out[:, points:]).T
        dq = jnp.where(upper, dq[:, :points], dq[:, points:]).T
        mixed[s, :, lanes] = jnp.where(live, out, 0.0).astype(BF16)
        dquery[mine, lanes] = (dq * 0.125).astype(BF16)
        dkeys[part, lanes] = dot(dscore, qq).astype(BF16)
        dvalues[part, lanes] = dot(prob, gg).astype(BF16)

    def gradients(which):
        side = pl.ds(pl.multiple_of(which * 256, 256), 256)
        of_query = None
        for s in range(slots):
            part = dot(turned[side, pl.ds(s * per, points)], dquery[pl.ds(s * points, points), :])
            of_query = part if of_query is None else of_query + part
        return dot(turned[side, :], dvalues[...]), of_query, dot(turned[side, :], dkeys[...])

    def sums():
        for p, part in enumerate(gradients(here.other)):
            away[p] = part.astype(BF16)
        first = [place[line] for line, _, _ in axes]
        row_of = [[pl.multiple_of((first[p] + k) % 4 * 64, 64) for k in (1, 2, 3, 0)] for p in range(3)]
        swaps = {}
        for p, k in pieces:
            at = pl.ds(row_of[p][k], 64)
            swaps[p, k] = send(away.at[p, at], from0.at[p, at], s0.at[p, k], r0.at[p, k], here.partner)
        for p, part in enumerate(gradients(core)):
            own[p] = part
        one = {}
        for p, k in pieces:
            at = pl.ds(row_of[p][k], 64)
            swaps[p, k].wait_recv()
            acc = own[p, at, :] + from0[p, at, :].astype(F32)
            if k < 3:
                half[p, at, :] = acc.astype(BF16)
                one[p, k] = send(half.at[p, at], from1.at[p, k], s1.at[p, k], r1.at[p, k], lines[p][k])
            else:
                own[p, at, :] = acc
        yield
        order = (1, 2, 0)
        for p in order:
            acc = own[p, pl.ds(row_of[p][3], 64), :]
            for k in range(3):
                one[p, k].wait_recv()
                acc = acc + from1[p, k].astype(F32)
            for j in range(4):
                part1[p, j] = acc[:, j * 128 : (j + 1) * 128].astype(BF16)
            _, u, v = axes[p]
            for n, (i, j) in enumerate(steps):
                a, b = (place[u] + i) % 4, (place[v] + j) % 4
                send(part1.at[p, b, pl.ds(a * 16, 16)], from2.at[p, n], s2.at[p], r2.at[p], planes[p][n])
        yield
        for p in order:
            flat_wait(from2.at[p], r2.at[p])
            _, u, v = axes[p]
            acc = part1[p, place[v], pl.ds(place[u] * 16, 16), :].astype(F32)
            for n in range(15):
                acc = acc + from2[p, n].astype(F32)
            tiles[zh, p] = acc.astype(BF16)
        three = [send(tiles.at[zh], tiles.at[zh], s3.at[k], r3.at[k], deep[k]) for k in range(3)]
        yield
        for copy in three:
            copy.wait_recv()
        for p in order:
            acc = tiles[0, p].astype(F32)
            for i in range(1, 4):
                acc = acc + tiles[i, p].astype(F32)
            _, u, v = axes[p]
            mine = summed.at[
                p,
                pl.ds(core * 256 + first[p] * 64 + place[u] * 16, 16),
                pl.ds(pl.multiple_of(place[v] * 128, 128), 128),
            ]
            mine[...] = acc.astype(BF16)
            for n in range(15):
                send(mine, mine, s4.at[p], r4.at[p], planes[p][n])
        yield
        five, six = {}, []
        for p in order:
            flat_wait(from2.at[p], r4.at[p])
            mine = summed.at[p, pl.ds(core * 256 + first[p] * 64, 64)]
            for k in range(3):
                five[p, k] = send(mine, mine, s5.at[p, k], r5.at[p, k], lines[p][k])
            six.append(send(mine, mine, s6.at[p, 3], r6.at[p, 3], here.partner))
        yield
        for k in (0, 2, 1):
            for p in order:
                five[p, k].wait_recv()
                mine = summed.at[p, pl.ds(core * 256 + (first[p] + 3 - k) % 4 * 64, 64)]
                six.append(send(mine, mine, s6.at[p, k], r6.at[p, k], here.partner))
        yield
        for copy in six:
            copy.wait()
        for p in range(3):
            flat_wait(from2.at[p], s2.at[p])
            flat_wait(from2.at[p], s4.at[p])
        for copy in [*swaps.values(), *one.values(), *three, *five.values()]:
            copy.wait_send()
        yield

    def terms():
        for s in range(slots):
            part = pl.ds(s * per, per)
            value = dot(dkeys[part, :], w_key[...], NT) + dot(dvalues[part, :], w_value[...], NT)
            term[pl.ds(s * entries, entries)] = value.reshape(entries, points, width)
        for t in range(5 * slots):
            acc = None
            for s in range(slots):
                number, at = 0, 0
                for m in reversed(range(entries)):
                    same = places[s][m] == t
                    number = number + jnp.where(same, 1, 0)
                    at = jnp.where(same, m, at)
                value = term[s * entries + at] * number.astype(F32)
                acc = value if acc is None else acc + value
            if t < slots:
                mine = dquery[pl.ds(t * points, points), :]
                own_grad[t] = acc + dot(mine, w_query[...], NT)
            else:
                far_grad[t - slots] = acc.astype(BF16)

    for pair in range(4):
        for s in range(slots):
            heads(s, pair)
    src = [far_grad.at[pl.ds(2 * d, 2)] for d in range(4)]
    dst = [back.at[d] for d in range(4)]
    chain = sums()
    next(chain)
    terms()
    for at in range(2, 7):
        next(chain)
        if at == RETURN_AT:
            exchange_start(here, src, dst, *behind)
        if at == RETURN_AT + 1:
            exchange_relay(here, src, dst, *behind)
    exchange_finish(here, src, dst, *behind)
    acc = own_grad[...]
    for d in range(4):
        acc = acc + back[d].astype(F32)
    feat_grad[...] = acc.astype(BF16)
    next(chain)


def layer(patch_count, point_count, neighbours, neighbour_points, feats, w_query, w_key, w_value, out_grad):
    slots, points, width = feats.shape
    entries = slots * (neighbours.shape[-1] + 1)
    own, every = slots * points, entries * points
    dma = pltpu.SemaphoreType.DMA
    smem = pl.BlockSpec(memory_space=pltpu.SMEM)
    vmem = pl.BlockSpec(memory_space=pltpu.VMEM)
    hbm = pl.BlockSpec(memory_space=pl.ANY)

    def held(*shape, kind=BF16):
        return pltpu.VMEM(shape, kind)

    return pl.pallas_call(
        layer_kernel,
        out_shape=[
            jax.ShapeDtypeStruct((slots, points, width), BF16),
            jax.ShapeDtypeStruct((slots, points, width), BF16),
            jax.ShapeDtypeStruct((3, 512, 512), BF16),
        ],
        in_specs=[smem] * 4 + [vmem] + [hbm] * 4,
        out_specs=[vmem] * 3,
        scratch_shapes=[
            held(width, width), held(width, width), held(width, width), held(slots, points, width),
            held(5 * slots, points, width),
            held(every, width),
            held(width, every),
            held(every, width), held(every, width),
            held(own, width), held(own, width),
            held(every, width), held(every, width),
            held(entries, points, width, kind=F32),
            held(slots, points, width, kind=F32),
            held(4 * slots, points, width),
            held(4, slots, points, width),
            held(3, 256, 512), held(3, 256, 512, kind=F32),
            held(3, 256, 512), held(3, 256, 512),
            held(3, 3, 64, 512), held(3, 4, 64, 128),
            held(3, 15, 16, 128), held(4, 3, 16, 128),
            dma((5,)),
            dma((3, 4)), dma((3, 4)),
            dma((3, 3)), dma((3, 3)),
            dma((3,)), dma((3,)),
            dma((3,)), dma((3,)),
            dma((3,)), dma((3,)),
            dma((3, 3)), dma((3, 3)),
            dma((3, 4)), dma((3, 4)),
            *EXCHANGE_SCRATCH,
            *EXCHANGE_SCRATCH,
        ],
        compiler_params=pltpu.CompilerParams(
            collective_id=0, has_side_effects=True, vmem_limit_bytes=VMEM_LIMIT
        ),
        name="layer",
    )(patch_count, point_count, neighbours, neighbour_points, feats, w_query, w_key, w_value, out_grad)


def finish_kernel(mixed, feat_grad, summed, *rest):
    outs, (rows, sums, arrive, leave) = rest[:5], rest[5:]
    groups = [[(summed.at[(i + 1) % 3], sums.at[i])] for i in range(3)]
    groups += [[(mixed, rows.at[0])], [(feat_grad, rows.at[1])]]
    held = [sums.at[0], sums.at[1], sums.at[2], rows.at[0], rows.at[1]]
    outs = [*outs[2:], *outs[:2]]
    loads, n = [], 0
    for group in groups:
        loads.append([])
        for src, dst in group:
            loads[-1].append(pltpu.make_async_copy(src, dst, arrive.at[n]))
            loads[-1][-1].start()
            n += 1
    stores = []
    for i, group in enumerate(loads):
        for copy in group:
            copy.wait()
        stores.append(pltpu.make_async_copy(held[i], outs[i], leave.at[i]))
        stores[-1].start()
    for copy in stores:
        copy.wait()


def finish(mixed, feat_grad, summed):
    hbm = pl.BlockSpec(memory_space=pl.ANY)
    width = mixed.shape[2]
    return pl.pallas_call(
        finish_kernel,
        out_shape=[jax.ShapeDtypeStruct(mixed.shape, BF16)] * 2
        + [jax.ShapeDtypeStruct((width, width), BF16)] * 3,
        in_specs=[hbm] * 3,
        out_specs=[hbm] * 5,
        scratch_shapes=[
            pltpu.VMEM((2, *mixed.shape), BF16),
            pltpu.VMEM((3, width, width), BF16),
            pltpu.SemaphoreType.DMA((5,)),
            pltpu.SemaphoreType.DMA((5,)),
        ],
        compiler_params=pltpu.CompilerParams(vmem_limit_bytes=VMEM_LIMIT),
        name="finish",
    )(mixed, feat_grad, summed)


def body(
    feats, w_query, w_key, w_value, out_grad, patch_count, point_count, neighbours, neighbour_points
):
    slots, points, width = (feats.shape[2], feats.shape[3], feats.shape[4])
    mixed, feat_grad, summed = layer(
        patch_count, point_count, neighbours, neighbour_points,
        feats.reshape(slots, points, width), w_query, w_key, w_value,
        out_grad.reshape(slots, points, width),
    )
    mixed, feat_grad, *sums = finish(mixed, feat_grad, summed)
    return (mixed.reshape(feats.shape), feat_grad.reshape(feats.shape), *sums)


def solution(mesh):
    return jax.shard_map(
        body,
        mesh=mesh,
        in_specs=(
            P("gx", "gy", None, None, None),
            P(),
            P(),
            P(),
            P("gx", "gy", None, None, None),
            P("gx", "gy"),
            P("gx", "gy", None),
            P("gx", "gy", None, None),
            P("gx", "gy", None, None),
        ),
        out_specs=(P("gx", "gy", None, None, None), P("gx", "gy", None, None, None), P(), P(), P()),
        check_vma=False,
    )
```

```python
import functools

import jax
import jax.numpy as jnp
from jax import lax
from jax.experimental import pallas as pl
from jax.experimental.pallas import tpu as pltpu
from jax.sharding import PartitionSpec as P

HEADS = 8
MESH = pl.DeviceIdType.MESH
VMEM_LIMIT = 56 * 1024 * 1024
F32 = jnp.float32
BF16 = jnp.bfloat16

NT = (((1,), (1,)), ((), ()))
TN = (((0,), (0,)), ((), ()))


def dot(a, b, dims=(((1,), (0,)), ((), ()))):
    return lax.dot_general(a, b, dims, preferred_element_type=F32)


def send(src, dst, send_sem, recv_sem, peer):
    copy = pltpu.make_async_remote_copy(
        src_ref=src,
        dst_ref=dst,
        send_sem=send_sem,
        recv_sem=recv_sem,
        device_id=peer,
        device_id_type=MESH,
    )
    copy.start()
    return copy


class Place:
    def __init__(self):
        a, b = lax.axis_index("gx"), lax.axis_index("gy")
        self.core, self.x, self.zh, self.y, self.zl = a % 2, (a // 2) % 4, a // 8, b // 4, b % 4
        self.other = 1 - self.core
        self.edge = self.x == 3 * self.core
        self.partner = self.at(core=self.other)
        self.outer = ((a + 31 + 2 * self.core) % 32, b)
        self.down, self.up = (a, (b + 15) % 16), (a, (b + 1) % 16)
        self.source = self.at(x=3 * self.core)
        self.final = self.at(core=self.other, x=3 * self.other, zh=(self.zh + 3 + 2 * self.core) % 4)
        self.reached = [
            self.at(core=self.other, x=p, zh=(self.zh + 3 + 2 * self.core) % 4) for p in range(4)
        ]
        self.turn = [(self.x + k) % 4 for k in range(1, 4)]

    def at(self, core=None, x=None, zh=None, y=None, zl=None):
        core = self.core if core is None else core
        x = self.x if x is None else x
        zh = self.zh if zh is None else zh
        y = self.y if y is None else y
        zl = self.zl if zl is None else zl
        return ((zh * 4 + x) * 2 + core, y * 4 + zl)


def signal(peers):
    barrier = pltpu.get_barrier_semaphore()
    for peer in peers:
        pl.semaphore_signal(barrier, inc=1, device_id=peer, device_id_type=MESH)


def greet(here, peers):
    barrier = pltpu.get_barrier_semaphore()
    peers = [here.partner, here.down, here.up, *peers]
    signal(peers)

    @pl.when(here.edge)
    def _():
        signal([here.at(x=p) for p in here.turn] + here.reached)
        pl.semaphore_wait(barrier, len(peers) + 7)

    @pl.when(jnp.logical_not(here.edge))
    def _():
        signal([here.source, here.final, here.outer])
        pl.semaphore_wait(barrier, len(peers) + 3)


def quarter(ref, p):
    if len(ref.shape) == 2:
        return ref.at[pl.ds(p * 32, 32)]
    return ref.at[p // 2, pl.ds(p % 2 * 64, 64)]


def flat_wait(ref, sem):
    pltpu.make_async_copy(ref, ref, sem).wait()


def exchange_scratch(rows):
    return [
        pltpu.VMEM((rows, 512), BF16),
        pltpu.SemaphoreType.DMA((4,)),
        pltpu.SemaphoreType.DMA((4,)),
        pltpu.SemaphoreType.DMA((4,)),
        pltpu.SemaphoreType.DMA((4,)),
        pltpu.SemaphoreType.DMA((2,)),
    ]


def exchange_start(here, src, dst, relay, s, r, sq, rq, hop):
    @pl.when(here.edge)
    def _():
        for p in here.turn:
            send(quarter(src[1], p), relay, sq.at[p], hop.at[0], here.at(x=p))
        send(quarter(src[1], here.x), quarter(dst[1], here.x), sq.at[here.x], rq.at[here.x], here.final)

    send(src[3], dst[2], s.at[3], r.at[2], here.up)
    send(src[2], dst[3], s.at[2], r.at[3], here.down)
    send(src[0], dst[0], s.at[0], r.at[0], here.partner)

    @pl.when(jnp.logical_not(here.edge))
    def _():
        send(src[1], dst[1], s.at[1], r.at[1], here.outer)


def exchange_relay(here, src, dst, relay, s, r, sq, rq, hop):
    @pl.when(jnp.logical_not(here.edge))
    def _():
        flat_wait(relay, hop.at[0])
        send(relay, quarter(dst[1], here.x), hop.at[1], rq.at[here.x], here.final)


def exchange_finish(here, src, dst, relay, s, r, sq, rq, hop):
    for d in (0, 2, 3):
        flat_wait(dst[d], r.at[d])

    @pl.when(here.edge)
    def _():
        for p in range(4):
            flat_wait(relay, rq.at[p])
        for p in range(4):
            flat_wait(relay, sq.at[p])

    @pl.when(jnp.logical_not(here.edge))
    def _():
        flat_wait(dst[1], r.at[1])
        flat_wait(src[1], s.at[1])
        flat_wait(relay, hop.at[1])

    for d in (0, 2, 3):
        flat_wait(src[d], s.at[d])


def side_of(code, even):
    swapped = jnp.where(code < 4, code + 2, code - 2)
    return jnp.where(even & (code >= 2) & (code < 6), swapped, code)


RETURN_AT = (2, 3)


def layer_kernel(
    patch_count, point_count, neighbours, neighbour_points,
    feats, w_query_hbm, w_key_hbm, w_value_hbm, out_grad_hbm,
    mixed, feat_grad, summed,
    w_query, w_key, w_value, out_grad,
    table, rows, turned, keys, values, query, dquery, dkeys, dvalues,
    term, own_grad, far_grad, back,
    away, own, from0, half, from1, part1, from2, tiles,
    loads, s0, r0, s1, r1, s2, r2, s3, r3, s4, r4, s5, r5, s6, r6,
    *scratch,
):
    slots, points, width = feats.shape
    near = neighbours.shape[-1]
    entries = near + 1
    per = entries * points
    here = Place()
    core, x, y, zh, zl = here.core, here.x, here.y, here.zh, here.zl
    axes = (("zl", "x", "y"), ("x", "y", "zl"), ("y", "x", "zl"))
    place = {"x": x, "y": y, "zl": zl, "zh": zh}

    def moved(**steps):
        return here.at(**{axis: (place[axis] + by) % 4 for axis, by in steps.items()})

    lines = [[moved(**{line: k}) for k in range(1, 4)] for line, _, _ in axes]
    steps = sorted(((i, j) for i in range(4) for j in range(4) if i + j), key=lambda t: -min(t[0], 4 - t[0]) - t[1])
    planes = [[moved(**{u: i, v: j}) for i, j in steps] for _, u, v in axes]
    deep = [moved(zh=k) for k in range(1, 4)]
    pieces = [(p, k) for k in range(4) for p in range(3)]
    ahead, *behind = (scratch[i : i + 6] for i in (0, 6, 12))

    started = []
    for n, (src, dst) in enumerate(
        [
            (w_query_hbm, w_query),
            (w_key_hbm, w_key),
            (w_value_hbm, w_value),
            (out_grad_hbm, out_grad),
            (feats, table.at[pl.ds(0, slots)]),
        ]
    ):
        started.append(pltpu.make_async_copy(src, dst, loads.at[n]))
        started[-1].start()
    crosswise = [
        moved(**{u: i, v: j}) for u, v in (("x", "y"), ("x", "zl"), ("y", "zl"))
        for i in range(1, 4) for j in range(1, 4)
    ]
    greet(here, [*lines[0], *lines[1], *lines[2], *deep, *crosswise])
    src = [feats] * 4
    dst = [table.at[pl.ds(2 + 2 * d, 2)] for d in range(4)]
    exchange_start(here, src, dst, *ahead)

    for copy in started:
        copy.wait()
    for s in range(slots):
        query[pl.ds(s * points, points), :] = dot(feats[s], w_query[...]).astype(BF16)
    for s in range(slots):
        part = pl.ds(s * per, points)
        rows[part, :] = feats[s]
        keys[part, :] = dot(feats[s], w_key[...]).astype(BF16)
        values[part, :] = dot(feats[s], w_value[...]).astype(BF16)
    exchange_relay(here, src, dst, *ahead)
    exchange_finish(here, src, dst, *ahead)

    even = core == 0
    places = []
    for s in range(slots):
        places.append([s] + [side_of(neighbours[0, 0, s, m], even) for m in range(near)])
        for m in range(1, entries):
            rows[pl.ds((s * entries + m) * points, points), :] = table[places[s][m]]
        part = pl.ds(s * per + points, near * points)
        keys[part, :] = dot(rows[part, :], w_key[...]).astype(BF16)
        values[part, :] = dot(rows[part, :], w_value[...]).astype(BF16)
        part = pl.ds(s * per, per)
        turned[:, part] = rows[part, :].T

    lane = lax.broadcasted_iota(jnp.int32, (points, 128), 1)
    row = lax.broadcasted_iota(jnp.int32, (points, 128), 0)
    low = lane < 64
    lives, biases = [], []
    for s in range(slots):
        count = jnp.where(s < patch_count[0, 0], point_count[0, 0, s], 0)
        lives.append(row < count)
        bias = []
        for m in range(entries):
            most = point_count[0, 0, s] if m == 0 else neighbour_points[0, 0, s, m - 1]
            bias.append(jnp.where((row >= most) & (lane == 0), -1e30, 0.0).astype(BF16))
        biases.append(jnp.concatenate(bias, axis=0))
    one = jnp.where(lax.broadcasted_iota(jnp.int32, (2 * points, 128), 1) == 0, 1.0, 0.0).astype(BF16)
    upper = lax.broadcasted_iota(jnp.int32, (128, points), 0) < 64

    def heads(s, pair):
        part = pl.ds(s * per, per)
        mine = pl.ds(s * points, points)
        lanes = pl.ds(pair * 128, 128)
        live = lives[s]
        kk = keys[part, lanes]
        vv = values[part, lanes]
        qq = query[mine, lanes].astype(F32) * 0.125
        gg = jnp.where(live, out_grad[s, :, lanes].astype(F32), 0.0)
        qq = jnp.concatenate([jnp.where(low, qq, 0.0), jnp.where(low, 0.0, qq)], axis=0).astype(BF16)
        gg = jnp.concatenate([jnp.where(low, gg, 0.0), jnp.where(low, 0.0, gg)], axis=0).astype(BF16)
        score = dot(jnp.concatenate([kk, biases[s]], axis=1), jnp.concatenate([qq, one], axis=1), NT)
        dprob = dot(vv, gg, NT)
        top = jnp.max(score, axis=0, keepdims=True)
        expo = jnp.exp(score - top)
        inverse = 1.0 / jnp.sum(expo, axis=0, keepdims=True)
        prob = expo * inverse
        inner = jnp.sum(prob * dprob, axis=0, keepdims=True)
        dscore = (prob * (dprob - inner)).astype(BF16)
        prob = prob.astype(BF16)
        out = dot(vv, prob, TN)
        dq = dot(kk, dscore, TN)
        out = jnp.where(upper, out[:, :points], out[:, points:]).T
        dq = jnp.where(upper, dq[:, :points], dq[:, points:]).T
        mixed[s, :, lanes] = jnp.where(live, out, 0.0).astype(BF16)
        dquery[mine, lanes] = (dq * 0.125).astype(BF16)
        dkeys[part, lanes] = dot(dscore, qq).astype(BF16)
        dvalues[part, lanes] = dot(prob, gg).astype(BF16)

    def gradients(which):
        side = pl.ds(pl.multiple_of(which * 256, 256), 256)
        of_query = None
        for s in range(slots):
            part = dot(turned[side, pl.ds(s * per, points)], dquery[pl.ds(s * points, points), :])
            of_query = part if of_query is None else of_query + part
        return dot(turned[side, :], dvalues[...]), of_query, dot(turned[side, :], dkeys[...])

    def sums():
        for p, part in enumerate(gradients(here.other)):
            away[p] = part.astype(BF16)
        first = [place[line] for line, _, _ in axes]
        row_of = [[pl.multiple_of((first[p] + k) % 4 * 64, 64) for k in (1, 2, 3, 0)] for p in range(3)]
        swaps = {}
        for p, k in pieces:
            at = pl.ds(row_of[p][k], 64)
            swaps[p, k] = send(away.at[p, at], from0.at[p, at], s0.at[p, k], r0.at[p, k], here.partner)
        for p, part in enumerate(gradients(core)):
            own[p] = part
        one = {}
        for p, k in pieces:
            at = pl.ds(row_of[p][k], 64)
            swaps[p, k].wait_recv()
            acc = own[p, at, :] + from0[p, at, :].astype(F32)
            if k < 3:
                half[p, at, :] = acc.astype(BF16)
                one[p, k] = send(half.at[p, at], from1.at[p, k], s1.at[p, k], r1.at[p, k], lines[p][k])
            else:
                own[p, at, :] = acc
        yield
        order = (1, 2, 0)
        for p in order:
            acc = own[p, pl.ds(row_of[p][3], 64), :]
            for k in range(3):
                one[p, k].wait_recv()
                acc = acc + from1[p, k].astype(F32)
            for j in range(4):
                part1[p, j] = acc[:, j * 128 : (j + 1) * 128].astype(BF16)
            _, u, v = axes[p]
            for n, (i, j) in enumerate(steps):
                a, b = (place[u] + i) % 4, (place[v] + j) % 4
                send(part1.at[p, b, pl.ds(a * 16, 16)], from2.at[p, n], s2.at[p], r2.at[p], planes[p][n])
        yield
        for p in order:
            flat_wait(from2.at[p], r2.at[p])
            _, u, v = axes[p]
            acc = part1[p, place[v], pl.ds(place[u] * 16, 16), :].astype(F32)
            for n in range(15):
                acc = acc + from2[p, n].astype(F32)
            tiles[zh, p] = acc.astype(BF16)
        three = [send(tiles.at[zh], tiles.at[zh], s3.at[k], r3.at[k], deep[k]) for k in range(3)]
        yield
        for copy in three:
            copy.wait_recv()
        for p in order:
            acc = tiles[0, p].astype(F32)
            for i in range(1, 4):
                acc = acc + tiles[i, p].astype(F32)
            _, u, v = axes[p]
            mine = summed.at[
                p,
                pl.ds(core * 256 + first[p] * 64 + place[u] * 16, 16),
                pl.ds(pl.multiple_of(place[v] * 128, 128), 128),
            ]
            mine[...] = acc.astype(BF16)
            for n in range(15):
                send(mine, mine, s4.at[p], r4.at[p], planes[p][n])
        yield
        five, six = {}, []
        for p in order:
            flat_wait(from2.at[p], r4.at[p])
            mine = summed.at[p, pl.ds(core * 256 + first[p] * 64, 64)]
            for k in range(3):
                five[p, k] = send(mine, mine, s5.at[p, k], r5.at[p, k], lines[p][k])
            six.append(send(mine, mine, s6.at[p, 3], r6.at[p, 3], here.partner))
        yield
        for k in (0, 2, 1):
            for p in order:
                five[p, k].wait_recv()
                mine = summed.at[p, pl.ds(core * 256 + (first[p] + 3 - k) % 4 * 64, 64)]
                six.append(send(mine, mine, s6.at[p, k], r6.at[p, k], here.partner))
        yield
        for copy in six:
            copy.wait()
        for p in range(3):
            flat_wait(from2.at[p], s2.at[p])
            flat_wait(from2.at[p], s4.at[p])
        for copy in [*swaps.values(), *one.values(), *three, *five.values()]:
            copy.wait_send()
        yield

    def terms():
        for s in range(slots):
            part = pl.ds(s * per, per)
            value = dot(dkeys[part, :], w_key[...], NT) + dot(dvalues[part, :], w_value[...], NT)
            term[pl.ds(s * entries, entries)] = value.reshape(entries, points, width)
        for t in range(5 * slots):
            acc = None
            for s in range(slots):
                number, at = 0, 0
                for m in reversed(range(entries)):
                    same = places[s][m] == t
                    number = number + jnp.where(same, 1, 0)
                    at = jnp.where(same, m, at)
                value = term[s * entries + at] * number.astype(F32)
                acc = value if acc is None else acc + value
            if t < slots:
                mine = dquery[pl.ds(t * points, points), :]
                own_grad[t] = acc + dot(mine, w_query[...], NT)
            else:
                far_grad[t - slots] = acc.astype(BF16)

    for pair in range(4):
        for s in range(slots):
            heads(s, pair)
    returns = [
        ([far_grad.at[2 * d + i] for d in range(4)], [back.at[d, i] for d in range(4)], *behind[i])
        for i in range(2)
    ]
    chain = sums()
    for at in range(1, 7):
        next(chain)
        if at == 1:
            terms()
        for i in range(2):
            if at == RETURN_AT[i]:
                exchange_start(here, *returns[i])
            if at == RETURN_AT[i] + 1:
                exchange_relay(here, *returns[i])
    for i in range(2):
        exchange_finish(here, *returns[i])
    acc = own_grad[...]
    for d in range(4):
        acc = acc + back[d].astype(F32)
    feat_grad[...] = acc.astype(BF16)
    next(chain)


def layer(patch_count, point_count, neighbours, neighbour_points, feats, w_query, w_key, w_value, out_grad):
    slots, points, width = feats.shape
    entries = slots * (neighbours.shape[-1] + 1)
    own, every = slots * points, entries * points
    dma = pltpu.SemaphoreType.DMA
    smem = pl.BlockSpec(memory_space=pltpu.SMEM)
    vmem = pl.BlockSpec(memory_space=pltpu.VMEM)
    hbm = pl.BlockSpec(memory_space=pl.ANY)

    def held(*shape, kind=BF16):
        return pltpu.VMEM(shape, kind)

    return pl.pallas_call(
        layer_kernel,
        out_shape=[
            jax.ShapeDtypeStruct((slots, points, width), BF16),
            jax.ShapeDtypeStruct((slots, points, width), BF16),
            jax.ShapeDtypeStruct((3, 512, 512), BF16),
        ],
        in_specs=[smem] * 4 + [vmem] + [hbm] * 4,
        out_specs=[vmem] * 3,
        scratch_shapes=[
            held(width, width), held(width, width), held(width, width), held(slots, points, width),
            held(5 * slots, points, width),
            held(every, width),
            held(width, every),
            held(every, width), held(every, width),
            held(own, width), held(own, width),
            held(every, width), held(every, width),
            held(entries, points, width, kind=F32),
            held(slots, points, width, kind=F32),
            held(4 * slots, points, width),
            held(4, slots, points, width),
            held(3, 256, 512), held(3, 256, 512, kind=F32),
            held(3, 256, 512), held(3, 256, 512),
            held(3, 3, 64, 512), held(3, 4, 64, 128),
            held(3, 15, 16, 128), held(4, 3, 16, 128),
            dma((5,)),
            dma((3, 4)), dma((3, 4)),
            dma((3, 3)), dma((3, 3)),
            dma((3,)), dma((3,)),
            dma((3,)), dma((3,)),
            dma((3,)), dma((3,)),
            dma((3, 3)), dma((3, 3)),
            dma((3, 4)), dma((3, 4)),
            *exchange_scratch(64),
            *exchange_scratch(32),
            *exchange_scratch(32),
        ],
        compiler_params=pltpu.CompilerParams(
            collective_id=0, has_side_effects=True, vmem_limit_bytes=VMEM_LIMIT
        ),
        name="layer",
    )(patch_count, point_count, neighbours, neighbour_points, feats, w_query, w_key, w_value, out_grad)


def finish_kernel(mixed, feat_grad, summed, *rest):
    outs, (rows, sums, arrive, leave) = rest[:5], rest[5:]
    groups = [[(summed.at[(i + 1) % 3], sums.at[i])] for i in range(3)]
    groups += [[(mixed, rows.at[0])], [(feat_grad, rows.at[1])]]
    held = [sums.at[0], sums.at[1], sums.at[2], rows.at[0], rows.at[1]]
    outs = [*outs[2:], *outs[:2]]
    loads, n = [], 0
    for group in groups:
        loads.append([])
        for src, dst in group:
            loads[-1].append(pltpu.make_async_copy(src, dst, arrive.at[n]))
            loads[-1][-1].start()
            n += 1
    stores = []
    for i, group in enumerate(loads):
        for copy in group:
            copy.wait()
        stores.append(pltpu.make_async_copy(held[i], outs[i], leave.at[i]))
        stores[-1].start()
    for copy in stores:
        copy.wait()


def finish(mixed, feat_grad, summed):
    hbm = pl.BlockSpec(memory_space=pl.ANY)
    width = mixed.shape[2]
    return pl.pallas_call(
        finish_kernel,
        out_shape=[jax.ShapeDtypeStruct(mixed.shape, BF16)] * 2
        + [jax.ShapeDtypeStruct((width, width), BF16)] * 3,
        in_specs=[hbm] * 3,
        out_specs=[hbm] * 5,
        scratch_shapes=[
            pltpu.VMEM((2, *mixed.shape), BF16),
            pltpu.VMEM((3, width, width), BF16),
            pltpu.SemaphoreType.DMA((5,)),
            pltpu.SemaphoreType.DMA((5,)),
        ],
        compiler_params=pltpu.CompilerParams(vmem_limit_bytes=VMEM_LIMIT),
        name="finish",
    )(mixed, feat_grad, summed)


def body(
    feats, w_query, w_key, w_value, out_grad, patch_count, point_count, neighbours, neighbour_points
):
    slots, points, width = (feats.shape[2], feats.shape[3], feats.shape[4])
    mixed, feat_grad, summed = layer(
        patch_count, point_count, neighbours, neighbour_points,
        feats.reshape(slots, points, width), w_query, w_key, w_value,
        out_grad.reshape(slots, points, width),
    )
    mixed, feat_grad, *sums = finish(mixed, feat_grad, summed)
    return (mixed.reshape(feats.shape), feat_grad.reshape(feats.shape), *sums)


def solution(mesh):
    return jax.shard_map(
        body,
        mesh=mesh,
        in_specs=(
            P("gx", "gy", None, None, None),
            P(),
            P(),
            P(),
            P("gx", "gy", None, None, None),
            P("gx", "gy"),
            P("gx", "gy", None),
            P("gx", "gy", None, None),
            P("gx", "gy", None, None),
        ),
        out_specs=(P("gx", "gy", None, None, None), P("gx", "gy", None, None, None), P(), P(), P()),
        check_vma=False,
    )
```

```python
import functools

import jax
import jax.numpy as jnp
from jax import lax
from jax.experimental import pallas as pl
from jax.experimental.pallas import tpu as pltpu
from jax.sharding import PartitionSpec as P

HEADS = 8
MESH = pl.DeviceIdType.MESH
VMEM_LIMIT = 56 * 1024 * 1024
F32 = jnp.float32
BF16 = jnp.bfloat16

NT = (((1,), (1,)), ((), ()))
TN = (((0,), (0,)), ((), ()))


def dot(a, b, dims=(((1,), (0,)), ((), ()))):
    return lax.dot_general(a, b, dims, preferred_element_type=F32)


def send(src, dst, send_sem, recv_sem, peer):
    copy = pltpu.make_async_remote_copy(
        src_ref=src,
        dst_ref=dst,
        send_sem=send_sem,
        recv_sem=recv_sem,
        device_id=peer,
        device_id_type=MESH,
    )
    copy.start()
    return copy


class Place:
    def __init__(self):
        a, b = lax.axis_index("gx"), lax.axis_index("gy")
        self.core, self.x, self.zh, self.y, self.zl = a % 2, (a // 2) % 4, a // 8, b // 4, b % 4
        self.other = 1 - self.core
        self.edge = self.x == 3 * self.core
        self.partner = self.at(core=self.other)
        self.outer = ((a + 31 + 2 * self.core) % 32, b)
        self.down, self.up = (a, (b + 15) % 16), (a, (b + 1) % 16)
        self.source = self.at(x=3 * self.core)
        self.final = self.at(core=self.other, x=3 * self.other, zh=(self.zh + 3 + 2 * self.core) % 4)
        self.reached = [
            self.at(core=self.other, x=p, zh=(self.zh + 3 + 2 * self.core) % 4) for p in range(4)
        ]
        self.turn = [(self.x + k) % 4 for k in range(1, 4)]

    def at(self, core=None, x=None, zh=None, y=None, zl=None):
        core = self.core if core is None else core
        x = self.x if x is None else x
        zh = self.zh if zh is None else zh
        y = self.y if y is None else y
        zl = self.zl if zl is None else zl
        return ((zh * 4 + x) * 2 + core, y * 4 + zl)


def signal(peers):
    barrier = pltpu.get_barrier_semaphore()
    for peer in peers:
        pl.semaphore_signal(barrier, inc=1, device_id=peer, device_id_type=MESH)


def greet(here, peers):
    barrier = pltpu.get_barrier_semaphore()
    peers = [here.partner, here.down, here.up, *peers]
    signal(peers)

    @pl.when(here.edge)
    def _():
        signal([here.at(x=p) for p in here.turn] + here.reached)
        pl.semaphore_wait(barrier, len(peers) + 7)

    @pl.when(jnp.logical_not(here.edge))
    def _():
        signal([here.source, here.final, here.outer])
        pl.semaphore_wait(barrier, len(peers) + 3)


def quarter(ref, p):
    if len(ref.shape) == 2:
        return ref.at[pl.ds(p * (ref.shape[0] // 4), ref.shape[0] // 4)]
    return ref.at[p // 2, pl.ds(p % 2 * 64, 64)]


def flat_wait(ref, sem):
    pltpu.make_async_copy(ref, ref, sem).wait()


def exchange_scratch(rows):
    return [
        pltpu.VMEM((rows, 512), BF16),
        pltpu.SemaphoreType.DMA((4,)),
        pltpu.SemaphoreType.DMA((4,)),
        pltpu.SemaphoreType.DMA((4,)),
        pltpu.SemaphoreType.DMA((4,)),
        pltpu.SemaphoreType.DMA((2,)),
    ]


def exchange_start(here, src, dst, relay, s, r, sq, rq, hop):
    @pl.when(here.edge)
    def _():
        for p in here.turn:
            send(quarter(src[1], p), relay, sq.at[p], hop.at[0], here.at(x=p))
        send(quarter(src[1], here.x), quarter(dst[1], here.x), sq.at[here.x], rq.at[here.x], here.final)

    send(src[3], dst[2], s.at[3], r.at[2], here.up)
    send(src[2], dst[3], s.at[2], r.at[3], here.down)
    send(src[0], dst[0], s.at[0], r.at[0], here.partner)

    @pl.when(jnp.logical_not(here.edge))
    def _():
        send(src[1], dst[1], s.at[1], r.at[1], here.outer)


def exchange_relay(here, src, dst, relay, s, r, sq, rq, hop):
    @pl.when(jnp.logical_not(here.edge))
    def _():
        flat_wait(relay, hop.at[0])
        send(relay, quarter(dst[1], here.x), hop.at[1], rq.at[here.x], here.final)


def exchange_finish(here, src, dst, relay, s, r, sq, rq, hop):
    for d in (0, 2, 3):
        flat_wait(dst[d], r.at[d])

    @pl.when(here.edge)
    def _():
        for p in range(4):
            flat_wait(relay, rq.at[p])
        for p in range(4):
            flat_wait(relay, sq.at[p])

    @pl.when(jnp.logical_not(here.edge))
    def _():
        flat_wait(dst[1], r.at[1])
        flat_wait(src[1], s.at[1])
        flat_wait(relay, hop.at[1])

    for d in (0, 2, 3):
        flat_wait(src[d], s.at[d])


def side_of(code, even):
    swapped = jnp.where(code < 4, code + 2, code - 2)
    return jnp.where(even & (code >= 2) & (code < 6), swapped, code)


RETURN_AT = (2, 2, 3, 4)


def layer_kernel(
    patch_count, point_count, neighbours, neighbour_points,
    feats, w_query_hbm, w_key_hbm, w_value_hbm, out_grad_hbm,
    mixed, feat_grad, summed,
    w_query, w_key, w_value, out_grad,
    table, rows, turned, keys, values, query, dquery, dkeys, dvalues,
    term, own_grad, far_grad, back,
    away, own, from0, half, from1, part1, from2, tiles,
    loads, s0, r0, s1, r1, s2, r2, s3, r3, s4, r4, s5, r5, s6, r6,
    *scratch,
):
    slots, points, width = feats.shape
    near = neighbours.shape[-1]
    entries = near + 1
    per = entries * points
    here = Place()
    core, x, y, zh, zl = here.core, here.x, here.y, here.zh, here.zl
    axes = (("zl", "x", "y"), ("x", "y", "zl"), ("y", "x", "zl"))
    place = {"x": x, "y": y, "zl": zl, "zh": zh}

    def moved(**steps):
        return here.at(**{axis: (place[axis] + by) % 4 for axis, by in steps.items()})

    lines = [[moved(**{line: k}) for k in range(1, 4)] for line, _, _ in axes]
    steps = sorted(((i, j) for i in range(4) for j in range(4) if i + j), key=lambda t: -min(t[0], 4 - t[0]) - t[1])
    planes = [[moved(**{u: i, v: j}) for i, j in steps] for _, u, v in axes]
    deep = [moved(zh=k) for k in range(1, 4)]
    pieces = [(p, k) for k in range(4) for p in range(3)]
    ahead, *behind = (scratch[i : i + 6] for i in range(0, 30, 6))

    started = []
    for n, (src, dst) in enumerate(
        [
            (w_query_hbm, w_query),
            (w_key_hbm, w_key),
            (w_value_hbm, w_value),
            (out_grad_hbm, out_grad),
            (feats, table.at[pl.ds(0, slots)]),
        ]
    ):
        started.append(pltpu.make_async_copy(src, dst, loads.at[n]))
        started[-1].start()
    crosswise = [
        moved(**{u: i, v: j}) for u, v in (("x", "y"), ("x", "zl"), ("y", "zl"))
        for i in range(1, 4) for j in range(1, 4)
    ]
    greet(here, [*lines[0], *lines[1], *lines[2], *deep, *crosswise])
    src = [feats] * 4
    dst = [table.at[pl.ds(2 + 2 * d, 2)] for d in range(4)]
    exchange_start(here, src, dst, *ahead)

    for copy in started:
        copy.wait()
    for s in range(slots):
        query[pl.ds(s * points, points), :] = dot(feats[s], w_query[...]).astype(BF16)
    for s in range(slots):
        part = pl.ds(s * per, points)
        rows[part, :] = feats[s]
        keys[part, :] = dot(feats[s], w_key[...]).astype(BF16)
        values[part, :] = dot(feats[s], w_value[...]).astype(BF16)
    exchange_relay(here, src, dst, *ahead)
    exchange_finish(here, src, dst, *ahead)

    even = core == 0
    places = []
    for s in range(slots):
        places.append([s] + [side_of(neighbours[0, 0, s, m], even) for m in range(near)])
        for m in range(1, entries):
            rows[pl.ds((s * entries + m) * points, points), :] = table[places[s][m]]
        part = pl.ds(s * per + points, near * points)
        keys[part, :] = dot(rows[part, :], w_key[...]).astype(BF16)
        values[part, :] = dot(rows[part, :], w_value[...]).astype(BF16)
        part = pl.ds(s * per, per)
        turned[:, part] = rows[part, :].T

    lane = lax.broadcasted_iota(jnp.int32, (points, 128), 1)
    row = lax.broadcasted_iota(jnp.int32, (points, 128), 0)
    low = lane < 64
    lives, biases = [], []
    for s in range(slots):
        count = jnp.where(s < patch_count[0, 0], point_count[0, 0, s], 0)
        lives.append(row < count)
        bias = []
        for m in range(entries):
            most = point_count[0, 0, s] if m == 0 else neighbour_points[0, 0, s, m - 1]
            bias.append(jnp.where((row >= most) & (lane == 0), -1e30, 0.0).astype(BF16))
        biases.append(jnp.concatenate(bias, axis=0))
    one = jnp.where(lax.broadcasted_iota(jnp.int32, (2 * points, 128), 1) == 0, 1.0, 0.0).astype(BF16)
    upper = lax.broadcasted_iota(jnp.int32, (128, points), 0) < 64

    def heads(s, pair):
        part = pl.ds(s * per, per)
        mine = pl.ds(s * points, points)
        lanes = pl.ds(pair * 128, 128)
        live = lives[s]
        kk = keys[part, lanes]
        vv = values[part, lanes]
        qq = query[mine, lanes].astype(F32) * 0.125
        gg = jnp.where(live, out_grad[s, :, lanes].astype(F32), 0.0)
        qq = jnp.concatenate([jnp.where(low, qq, 0.0), jnp.where(low, 0.0, qq)], axis=0).astype(BF16)
        gg = jnp.concatenate([jnp.where(low, gg, 0.0), jnp.where(low, 0.0, gg)], axis=0).astype(BF16)
        score = dot(jnp.concatenate([kk, biases[s]], axis=1), jnp.concatenate([qq, one], axis=1), NT)
        dprob = dot(vv, gg, NT)
        top = jnp.max(score, axis=0, keepdims=True)
        expo = jnp.exp(score - top)
        inverse = 1.0 / jnp.sum(expo, axis=0, keepdims=True)
        prob = expo * inverse
        inner = jnp.sum(prob * dprob, axis=0, keepdims=True)
        dscore = (prob * (dprob - inner)).astype(BF16)
        prob = prob.astype(BF16)
        out = dot(vv, prob, TN)
        dq = dot(kk, dscore, TN)
        out = jnp.where(upper, out[:, :points], out[:, points:]).T
        dq = jnp.where(upper, dq[:, :points], dq[:, points:]).T
        mixed[s, :, lanes] = jnp.where(live, out, 0.0).astype(BF16)
        dquery[mine, lanes] = (dq * 0.125).astype(BF16)
        dkeys[part, lanes] = dot(dscore, qq).astype(BF16)
        dvalues[part, lanes] = dot(prob, gg).astype(BF16)

    def gradients(which):
        side = pl.ds(pl.multiple_of(which * 256, 256), 256)
        of_query = None
        for s in range(slots):
            part = dot(turned[side, pl.ds(s * per, points)], dquery[pl.ds(s * points, points), :])
            of_query = part if of_query is None else of_query + part
        return dot(turned[side, :], dvalues[...]), of_query, dot(turned[side, :], dkeys[...])

    def sums():
        for p, part in enumerate(gradients(here.other)):
            away[p] = part.astype(BF16)
        first = [place[line] for line, _, _ in axes]
        row_of = [[pl.multiple_of((first[p] + k) % 4 * 64, 64) for k in (1, 2, 3, 0)] for p in range(3)]
        swaps = {}
        for p, k in pieces:
            at = pl.ds(row_of[p][k], 64)
            swaps[p, k] = send(away.at[p, at], from0.at[p, at], s0.at[p, k], r0.at[p, k], here.partner)
        for p, part in enumerate(gradients(core)):
            own[p] = part
        one = {}
        for p, k in pieces:
            at = pl.ds(row_of[p][k], 64)
            swaps[p, k].wait_recv()
            acc = own[p, at, :] + from0[p, at, :].astype(F32)
            if k < 3:
                half[p, at, :] = acc.astype(BF16)
                one[p, k] = send(half.at[p, at], from1.at[p, k], s1.at[p, k], r1.at[p, k], lines[p][k])
            else:
                own[p, at, :] = acc
        yield
        order = (1, 2, 0)
        for p in order:
            acc = own[p, pl.ds(row_of[p][3], 64), :]
            for k in range(3):
                one[p, k].wait_recv()
                acc = acc + from1[p, k].astype(F32)
            for j in range(4):
                part1[p, j] = acc[:, j * 128 : (j + 1) * 128].astype(BF16)
            _, u, v = axes[p]
            for n, (i, j) in enumerate(steps):
                a, b = (place[u] + i) % 4, (place[v] + j) % 4
                send(part1.at[p, b, pl.ds(a * 16, 16)], from2.at[p, n], s2.at[p], r2.at[p], planes[p][n])
        yield
        for p in order:
            flat_wait(from2.at[p], r2.at[p])
            _, u, v = axes[p]
            acc = part1[p, place[v], pl.ds(place[u] * 16, 16), :].astype(F32)
            for n in range(15):
                acc = acc + from2[p, n].astype(F32)
            tiles[zh, p] = acc.astype(BF16)
        three = [send(tiles.at[zh], tiles.at[zh], s3.at[k], r3.at[k], deep[k]) for k in range(3)]
        yield
        for copy in three:
            copy.wait_recv()
        for p in order:
            acc = tiles[0, p].astype(F32)
            for i in range(1, 4):
                acc = acc + tiles[i, p].astype(F32)
            _, u, v = axes[p]
            mine = summed.at[
                p,
                pl.ds(core * 256 + first[p] * 64 + place[u] * 16, 16),
                pl.ds(pl.multiple_of(place[v] * 128, 128), 128),
            ]
            mine[...] = acc.astype(BF16)
            for n in range(15):
                send(mine, mine, s4.at[p], r4.at[p], planes[p][n])
        yield
        five, six = {}, []
        for p in order:
            flat_wait(from2.at[p], r4.at[p])
            mine = summed.at[p, pl.ds(core * 256 + first[p] * 64, 64)]
            for k in range(3):
                five[p, k] = send(mine, mine, s5.at[p, k], r5.at[p, k], lines[p][k])
            six.append(send(mine, mine, s6.at[p, 3], r6.at[p, 3], here.partner))
        yield
        for k in (0, 2, 1):
            for p in order:
                five[p, k].wait_recv()
                mine = summed.at[p, pl.ds(core * 256 + (first[p] + 3 - k) % 4 * 64, 64)]
                six.append(send(mine, mine, s6.at[p, k], r6.at[p, k], here.partner))
        yield
        for copy in six:
            copy.wait()
        for p in range(3):
            flat_wait(from2.at[p], s2.at[p])
            flat_wait(from2.at[p], s4.at[p])
        for copy in [*swaps.values(), *one.values(), *three, *five.values()]:
            copy.wait_send()
        yield

    def terms():
        for s in range(slots):
            part = pl.ds(s * per, per)
            value = dot(dkeys[part, :], w_key[...], NT) + dot(dvalues[part, :], w_value[...], NT)
            term[pl.ds(s * entries, entries)] = value.reshape(entries, points, width)
        for t in range(5 * slots):
            acc = None
            for s in range(slots):
                number, at = 0, 0
                for m in reversed(range(entries)):
                    same = places[s][m] == t
                    number = number + jnp.where(same, 1, 0)
                    at = jnp.where(same, m, at)
                value = term[s * entries + at] * number.astype(F32)
                acc = value if acc is None else acc + value
            if t < slots:
                mine = dquery[pl.ds(t * points, points), :]
                own_grad[t] = acc + dot(mine, w_query[...], NT)
            else:
                far_grad[t - slots] = acc.astype(BF16)

    for pair in range(4):
        for s in range(slots):
            heads(s, pair)
    returns = []
    for i in range(4):
        part = pl.ds(i % 2 * 64, 64)
        returns.append(
            (
                [far_grad.at[2 * d + i // 2, part] for d in range(4)],
                [back.at[d, i // 2, part] for d in range(4)],
                *behind[i],
            )
        )
    chain = sums()
    for at in range(1, 7):
        next(chain)
        if at == 1:
            terms()
        for i in range(4):
            if at == RETURN_AT[i]:
                exchange_start(here, *returns[i])
            if at == RETURN_AT[i] + 1:
                exchange_relay(here, *returns[i])
    for i in range(4):
        exchange_finish(here, *returns[i])
    acc = own_grad[...]
    for d in range(4):
        acc = acc + back[d].astype(F32)
    feat_grad[...] = acc.astype(BF16)
    next(chain)


def layer(patch_count, point_count, neighbours, neighbour_points, feats, w_query, w_key, w_value, out_grad):
    slots, points, width = feats.shape
    entries = slots * (neighbours.shape[-1] + 1)
    own, every = slots * points, entries * points
    dma = pltpu.SemaphoreType.DMA
    smem = pl.BlockSpec(memory_space=pltpu.SMEM)
    vmem = pl.BlockSpec(memory_space=pltpu.VMEM)
    hbm = pl.BlockSpec(memory_space=pl.ANY)

    def held(*shape, kind=BF16):
        return pltpu.VMEM(shape, kind)

    return pl.pallas_call(
        layer_kernel,
        out_shape=[
            jax.ShapeDtypeStruct((slots, points, width), BF16),
            jax.ShapeDtypeStruct((slots, points, width), BF16),
            jax.ShapeDtypeStruct((3, 512, 512), BF16),
        ],
        in_specs=[smem] * 4 + [vmem] + [hbm] * 4,
        out_specs=[vmem] * 3,
        scratch_shapes=[
            held(width, width), held(width, width), held(width, width), held(slots, points, width),
            held(5 * slots, points, width),
            held(every, width),
            held(width, every),
            held(every, width), held(every, width),
            held(own, width), held(own, width),
            held(every, width), held(every, width),
            held(entries, points, width, kind=F32),
            held(slots, points, width, kind=F32),
            held(4 * slots, points, width),
            held(4, slots, points, width),
            held(3, 256, 512), held(3, 256, 512, kind=F32),
            held(3, 256, 512), held(3, 256, 512),
            held(3, 3, 64, 512), held(3, 4, 64, 128),
            held(3, 15, 16, 128), held(4, 3, 16, 128),
            dma((5,)),
            dma((3, 4)), dma((3, 4)),
            dma((3, 3)), dma((3, 3)),
            dma((3,)), dma((3,)),
            dma((3,)), dma((3,)),
            dma((3,)), dma((3,)),
            dma((3, 3)), dma((3, 3)),
            dma((3, 4)), dma((3, 4)),
            *exchange_scratch(64),
            *exchange_scratch(16),
            *exchange_scratch(16),
            *exchange_scratch(16),
            *exchange_scratch(16),
        ],
        compiler_params=pltpu.CompilerParams(
            collective_id=0, has_side_effects=True, vmem_limit_bytes=VMEM_LIMIT
        ),
        name="layer",
    )(patch_count, point_count, neighbours, neighbour_points, feats, w_query, w_key, w_value, out_grad)


def finish_kernel(mixed, feat_grad, summed, *rest):
    outs, (rows, sums, arrive, leave) = rest[:5], rest[5:]
    groups = [[(summed.at[(i + 1) % 3], sums.at[i])] for i in range(3)]
    groups += [[(mixed, rows.at[0])], [(feat_grad, rows.at[1])]]
    held = [sums.at[0], sums.at[1], sums.at[2], rows.at[0], rows.at[1]]
    outs = [*outs[2:], *outs[:2]]
    loads, n = [], 0
    for group in groups:
        loads.append([])
        for src, dst in group:
            loads[-1].append(pltpu.make_async_copy(src, dst, arrive.at[n]))
            loads[-1][-1].start()
            n += 1
    stores = []
    for i, group in enumerate(loads):
        for copy in group:
            copy.wait()
        stores.append(pltpu.make_async_copy(held[i], outs[i], leave.at[i]))
        stores[-1].start()
    for copy in stores:
        copy.wait()


def finish(mixed, feat_grad, summed):
    hbm = pl.BlockSpec(memory_space=pl.ANY)
    width = mixed.shape[2]
    return pl.pallas_call(
        finish_kernel,
        out_shape=[jax.ShapeDtypeStruct(mixed.shape, BF16)] * 2
        + [jax.ShapeDtypeStruct((width, width), BF16)] * 3,
        in_specs=[hbm] * 3,
        out_specs=[hbm] * 5,
        scratch_shapes=[
            pltpu.VMEM((2, *mixed.shape), BF16),
            pltpu.VMEM((3, width, width), BF16),
            pltpu.SemaphoreType.DMA((5,)),
            pltpu.SemaphoreType.DMA((5,)),
        ],
        compiler_params=pltpu.CompilerParams(vmem_limit_bytes=VMEM_LIMIT),
        name="finish",
    )(mixed, feat_grad, summed)


def body(
    feats, w_query, w_key, w_value, out_grad, patch_count, point_count, neighbours, neighbour_points
):
    slots, points, width = (feats.shape[2], feats.shape[3], feats.shape[4])
    mixed, feat_grad, summed = layer(
        patch_count, point_count, neighbours, neighbour_points,
        feats.reshape(slots, points, width), w_query, w_key, w_value,
        out_grad.reshape(slots, points, width),
    )
    mixed, feat_grad, *sums = finish(mixed, feat_grad, summed)
    return (mixed.reshape(feats.shape), feat_grad.reshape(feats.shape), *sums)


def solution(mesh):
    return jax.shard_map(
        body,
        mesh=mesh,
        in_specs=(
            P("gx", "gy", None, None, None),
            P(),
            P(),
            P(),
            P("gx", "gy", None, None, None),
            P("gx", "gy"),
            P("gx", "gy", None),
            P("gx", "gy", None, None),
            P("gx", "gy", None, None),
        ),
        out_specs=(P("gx", "gy", None, None, None), P("gx", "gy", None, None, None), P(), P(), P()),
        check_vma=False,
    )
```

```python
import functools

import jax
import jax.numpy as jnp
from jax import lax
from jax.experimental import pallas as pl
from jax.experimental.pallas import tpu as pltpu
from jax.sharding import PartitionSpec as P

HEADS = 8
MESH = pl.DeviceIdType.MESH
VMEM_LIMIT = 56 * 1024 * 1024
F32 = jnp.float32
BF16 = jnp.bfloat16

NT = (((1,), (1,)), ((), ()))
TN = (((0,), (0,)), ((), ()))


def dot(a, b, dims=(((1,), (0,)), ((), ()))):
    return lax.dot_general(a, b, dims, preferred_element_type=F32)


def send(src, dst, send_sem, recv_sem, peer):
    copy = pltpu.make_async_remote_copy(
        src_ref=src,
        dst_ref=dst,
        send_sem=send_sem,
        recv_sem=recv_sem,
        device_id=peer,
        device_id_type=MESH,
    )
    copy.start()
    return copy


class Place:
    def __init__(self):
        a, b = lax.axis_index("gx"), lax.axis_index("gy")
        self.core, self.x, self.zh, self.y, self.zl = a % 2, (a // 2) % 4, a // 8, b // 4, b % 4
        self.other = 1 - self.core
        self.edge = self.x == 3 * self.core
        self.partner = self.at(core=self.other)
        self.outer = ((a + 31 + 2 * self.core) % 32, b)
        self.down, self.up = (a, (b + 15) % 16), (a, (b + 1) % 16)
        self.source = self.at(x=3 * self.core)
        self.final = self.at(core=self.other, x=3 * self.other, zh=(self.zh + 3 + 2 * self.core) % 4)
        self.reached = [
            self.at(core=self.other, x=p, zh=(self.zh + 3 + 2 * self.core) % 4) for p in range(4)
        ]
        self.turn = [(self.x + k) % 4 for k in range(1, 4)]

    def at(self, core=None, x=None, zh=None, y=None, zl=None):
        core = self.core if core is None else core
        x = self.x if x is None else x
        zh = self.zh if zh is None else zh
        y = self.y if y is None else y
        zl = self.zl if zl is None else zl
        return ((zh * 4 + x) * 2 + core, y * 4 + zl)


def signal(peers):
    barrier = pltpu.get_barrier_semaphore()
    for peer in peers:
        pl.semaphore_signal(barrier, inc=1, device_id=peer, device_id_type=MESH)


def greet(here, peers):
    barrier = pltpu.get_barrier_semaphore()
    peers = [*peers, here.down, here.up, here.partner]
    signal(peers)

    @pl.when(here.edge)
    def _():
        signal([here.at(x=p) for p in here.turn] + here.reached)
        pl.semaphore_wait(barrier, len(peers) + 7)

    @pl.when(jnp.logical_not(here.edge))
    def _():
        signal([here.source, here.final, here.outer])
        pl.semaphore_wait(barrier, len(peers) + 3)


def quarter(ref, p):
    if len(ref.shape) == 2:
        return ref.at[pl.ds(p * (ref.shape[0] // 4), ref.shape[0] // 4)]
    return ref.at[p // 2, pl.ds(p % 2 * 64, 64)]


def flat_wait(ref, sem):
    pltpu.make_async_copy(ref, ref, sem).wait()


def exchange_scratch(rows):
    return [
        pltpu.VMEM((rows, 512), BF16),
        pltpu.SemaphoreType.DMA((4,)),
        pltpu.SemaphoreType.DMA((4,)),
        pltpu.SemaphoreType.DMA((4,)),
        pltpu.SemaphoreType.DMA((4,)),
        pltpu.SemaphoreType.DMA((2,)),
    ]


def exchange_start(here, src, dst, relay, s, r, sq, rq, hop):
    @pl.when(here.edge)
    def _():
        for p in here.turn:
            send(quarter(src[1], p), relay, sq.at[p], hop.at[0], here.at(x=p))
        send(quarter(src[1], here.x), quarter(dst[1], here.x), sq.at[here.x], rq.at[here.x], here.final)

    send(src[3], dst[2], s.at[3], r.at[2], here.up)
    send(src[2], dst[3], s.at[2], r.at[3], here.down)
    send(src[0], dst[0], s.at[0], r.at[0], here.partner)

    @pl.when(jnp.logical_not(here.edge))
    def _():
        send(src[1], dst[1], s.at[1], r.at[1], here.outer)


def exchange_relay(here, src, dst, relay, s, r, sq, rq, hop):
    @pl.when(jnp.logical_not(here.edge))
    def _():
        flat_wait(relay, hop.at[0])
        send(relay, quarter(dst[1], here.x), hop.at[1], rq.at[here.x], here.final)


def exchange_finish(here, src, dst, relay, s, r, sq, rq, hop):
    for d in (0, 2, 3):
        flat_wait(dst[d], r.at[d])

    @pl.when(here.edge)
    def _():
        for p in range(4):
            flat_wait(relay, rq.at[p])
        for p in range(4):
            flat_wait(relay, sq.at[p])

    @pl.when(jnp.logical_not(here.edge))
    def _():
        flat_wait(dst[1], r.at[1])
        flat_wait(src[1], s.at[1])
        flat_wait(relay, hop.at[1])

    for d in (0, 2, 3):
        flat_wait(src[d], s.at[d])


def side_of(code, even):
    swapped = jnp.where(code < 4, code + 2, code - 2)
    return jnp.where(even & (code >= 2) & (code < 6), swapped, code)


RETURN_AT = (2, 2, 3, 4)


def layer_kernel(
    patch_count, point_count, neighbours, neighbour_points,
    feats, w_query_hbm, w_key_hbm, w_value_hbm, out_grad_hbm,
    mixed, feat_grad, summed,
    w_query, w_key, w_value, out_grad,
    table, rows, turned, keys, values, query, dquery, dkeys, dvalues,
    term, own_grad, far_grad, back,
    away, own, from0, half, from1, part1, from2, tiles,
    loads, s0, r0, s1, r1, s2, r2, s3, r3, s4, r4, s5, r5, s6, r6,
    *scratch,
):
    slots, points, width = feats.shape
    near = neighbours.shape[-1]
    entries = near + 1
    per = entries * points
    here = Place()
    core, x, y, zh, zl = here.core, here.x, here.y, here.zh, here.zl
    axes = (("zl", "x", "y"), ("x", "y", "zl"), ("y", "x", "zl"))
    place = {"x": x, "y": y, "zl": zl, "zh": zh}

    def moved(**steps):
        return here.at(**{axis: (place[axis] + by) % 4 for axis, by in steps.items()})

    lines = [[moved(**{line: k}) for k in range(1, 4)] for line, _, _ in axes]
    steps = sorted(((i, j) for i in range(4) for j in range(4) if i + j), key=lambda t: -min(t[0], 4 - t[0]) - t[1])
    planes = [[moved(**{u: i, v: j}) for i, j in steps] for _, u, v in axes]
    deep = [moved(zh=k) for k in range(1, 4)]
    pieces = [(p, k) for k in range(4) for p in range(3)]
    ahead, *behind = (scratch[i : i + 6] for i in range(0, 30, 6))

    started = []
    for n, (src, dst) in enumerate(
        [
            (w_query_hbm, w_query),
            (w_key_hbm, w_key),
            (w_value_hbm, w_value),
            (out_grad_hbm, out_grad),
            (feats, table.at[pl.ds(0, slots)]),
        ]
    ):
        started.append(pltpu.make_async_copy(src, dst, loads.at[n]))
        started[-1].start()
    crosswise = [
        moved(**{u: i, v: j}) for u, v in (("x", "y"), ("x", "zl"), ("y", "zl"))
        for i in range(1, 4) for j in range(1, 4)
    ]
    greet(here, [*deep[1:2], *deep[0:1], *deep[2:], *reversed(crosswise), *lines[0], *lines[1], *lines[2]])
    src = [feats] * 4
    dst = [table.at[pl.ds(2 + 2 * d, 2)] for d in range(4)]
    exchange_start(here, src, dst, *ahead)

    for copy in started:
        copy.wait()
    for s in range(slots):
        query[pl.ds(s * points, points), :] = dot(feats[s], w_query[...]).astype(BF16)
    for s in range(slots):
        part = pl.ds(s * per, points)
        rows[part, :] = feats[s]
        keys[part, :] = dot(feats[s], w_key[...]).astype(BF16)
        values[part, :] = dot(feats[s], w_value[...]).astype(BF16)
    exchange_relay(here, src, dst, *ahead)
    exchange_finish(here, src, dst, *ahead)

    even = core == 0
    places = []
    for s in range(slots):
        places.append([s] + [side_of(neighbours[0, 0, s, m], even) for m in range(near)])
        for m in range(1, entries):
            rows[pl.ds((s * entries + m) * points, points), :] = table[places[s][m]]
        part = pl.ds(s * per + points, near * points)
        keys[part, :] = dot(rows[part, :], w_key[...]).astype(BF16)
        values[part, :] = dot(rows[part, :], w_value[...]).astype(BF16)
        part = pl.ds(s * per, per)
        turned[:, part] = rows[part, :].T

    lane = lax.broadcasted_iota(jnp.int32, (points, 128), 1)
    row = lax.broadcasted_iota(jnp.int32, (points, 128), 0)
    low = lane < 64
    lives, biases = [], []
    for s in range(slots):
        count = jnp.where(s < patch_count[0, 0], point_count[0, 0, s], 0)
        lives.append(row < count)
        bias = []
        for m in range(entries):
            most = point_count[0, 0, s] if m == 0 else neighbour_points[0, 0, s, m - 1]
            bias.append(jnp.where((row >= most) & (lane == 0), -1e30, 0.0).astype(BF16))
        biases.append(jnp.concatenate(bias, axis=0))
    one = jnp.where(lax.broadcasted_iota(jnp.int32, (2 * points, 128), 1) == 0, 1.0, 0.0).astype(BF16)
    upper = lax.broadcasted_iota(jnp.int32, (128, points), 0) < 64

    def heads(s, pair):
        part = pl.ds(s * per, per)
        mine = pl.ds(s * points, points)
        lanes = pl.ds(pair * 128, 128)
        live = lives[s]
        kk = keys[part, lanes]
        vv = values[part, lanes]
        qq = query[mine, lanes].astype(F32) * 0.125
        gg = jnp.where(live, out_grad[s, :, lanes].astype(F32), 0.0)
        qq = jnp.concatenate([jnp.where(low, qq, 0.0), jnp.where(low, 0.0, qq)], axis=0).astype(BF16)
        gg = jnp.concatenate([jnp.where(low, gg, 0.0), jnp.where(low, 0.0, gg)], axis=0).astype(BF16)
        score = dot(jnp.concatenate([kk, biases[s]], axis=1), jnp.concatenate([qq, one], axis=1), NT)
        dprob = dot(vv, gg, NT)
        top = jnp.max(score, axis=0, keepdims=True)
        expo = jnp.exp(score - top)
        inverse = 1.0 / jnp.sum(expo, axis=0, keepdims=True)
        prob = expo * inverse
        inner = jnp.sum(prob * dprob, axis=0, keepdims=True)
        dscore = (prob * (dprob - inner)).astype(BF16)
        prob = prob.astype(BF16)
        out = dot(vv, prob, TN)
        dq = dot(kk, dscore, TN)
        out = jnp.where(upper, out[:, :points], out[:, points:]).T
        dq = jnp.where(upper, dq[:, :points], dq[:, points:]).T
        mixed[s, :, lanes] = jnp.where(live, out, 0.0).astype(BF16)
        dquery[mine, lanes] = (dq * 0.125).astype(BF16)
        dkeys[part, lanes] = dot(dscore, qq).astype(BF16)
        dvalues[part, lanes] = dot(prob, gg).astype(BF16)

    def gradients(which):
        side = pl.ds(pl.multiple_of(which * 256, 256), 256)
        of_query = None
        for s in range(slots):
            part = dot(turned[side, pl.ds(s * per, points)], dquery[pl.ds(s * points, points), :])
            of_query = part if of_query is None else of_query + part
        return dot(turned[side, :], dvalues[...]), of_query, dot(turned[side, :], dkeys[...])

    def sums():
        for p, part in enumerate(gradients(here.other)):
            away[p] = part.astype(BF16)
        first = [place[line] for line, _, _ in axes]
        row_of = [[pl.multiple_of((first[p] + k) % 4 * 64, 64) for k in (1, 2, 3, 0)] for p in range(3)]
        swaps = {}
        for p, k in pieces:
            at = pl.ds(row_of[p][k], 64)
            swaps[p, k] = send(away.at[p, at], from0.at[p, at], s0.at[p, k], r0.at[p, k], here.partner)
        for p, part in enumerate(gradients(core)):
            own[p] = part
        one = {}
        for p, k in pieces:
            at = pl.ds(row_of[p][k], 64)
            swaps[p, k].wait_recv()
            acc = own[p, at, :] + from0[p, at, :].astype(F32)
            if k < 3:
                half[p, at, :] = acc.astype(BF16)
                one[p, k] = send(half.at[p, at], from1.at[p, k], s1.at[p, k], r1.at[p, k], lines[p][k])
            else:
                own[p, at, :] = acc
        yield
        order = (1, 2, 0)
        for p in order:
            acc = own[p, pl.ds(row_of[p][3], 64), :]
            for k in range(3):
                one[p, k].wait_recv()
                acc = acc + from1[p, k].astype(F32)
            for j in range(4):
                part1[p, j] = acc[:, j * 128 : (j + 1) * 128].astype(BF16)
            _, u, v = axes[p]
            for n, (i, j) in enumerate(steps):
                a, b = (place[u] + i) % 4, (place[v] + j) % 4
                send(part1.at[p, b, pl.ds(a * 16, 16)], from2.at[p, n], s2.at[p], r2.at[p], planes[p][n])
        yield
        for p in order:
            flat_wait(from2.at[p], r2.at[p])
            _, u, v = axes[p]
            acc = part1[p, place[v], pl.ds(place[u] * 16, 16), :].astype(F32)
            for n in range(15):
                acc = acc + from2[p, n].astype(F32)
            tiles[zh, p] = acc.astype(BF16)
        three = [send(tiles.at[zh], tiles.at[zh], s3.at[k], r3.at[k], deep[k]) for k in range(3)]
        yield
        for copy in three:
            copy.wait_recv()
        for p in order:
            acc = tiles[0, p].astype(F32)
            for i in range(1, 4):
                acc = acc + tiles[i, p].astype(F32)
            _, u, v = axes[p]
            mine = summed.at[
                p,
                pl.ds(core * 256 + first[p] * 64 + place[u] * 16, 16),
                pl.ds(pl.multiple_of(place[v] * 128, 128), 128),
            ]
            mine[...] = acc.astype(BF16)
            for n in range(15):
                send(mine, mine, s4.at[p], r4.at[p], planes[p][n])
        yield
        five, six = {}, []
        for p in order:
            flat_wait(from2.at[p], r4.at[p])
            mine = summed.at[p, pl.ds(core * 256 + first[p] * 64, 64)]
            for k in range(3):
                five[p, k] = send(mine, mine, s5.at[p, k], r5.at[p, k], lines[p][k])
            six.append(send(mine, mine, s6.at[p, 3], r6.at[p, 3], here.partner))
        yield
        for k in (0, 2, 1):
            for p in order:
                five[p, k].wait_recv()
                mine = summed.at[p, pl.ds(core * 256 + (first[p] + 3 - k) % 4 * 64, 64)]
                six.append(send(mine, mine, s6.at[p, k], r6.at[p, k], here.partner))
        yield
        for copy in six:
            copy.wait()
        for p in range(3):
            flat_wait(from2.at[p], s2.at[p])
            flat_wait(from2.at[p], s4.at[p])
        for copy in [*swaps.values(), *one.values(), *three, *five.values()]:
            copy.wait_send()
        yield

    def terms():
        for s in range(slots):
            part = pl.ds(s * per, per)
            value = dot(dkeys[part, :], w_key[...], NT) + dot(dvalues[part, :], w_value[...], NT)
            term[pl.ds(s * entries, entries)] = value.reshape(entries, points, width)
        for t in range(5 * slots):
            acc = None
            for s in range(slots):
                number, at = 0, 0
                for m in reversed(range(entries)):
                    same = places[s][m] == t
                    number = number + jnp.where(same, 1, 0)
                    at = jnp.where(same, m, at)
                value = term[s * entries + at] * number.astype(F32)
                acc = value if acc is None else acc + value
            if t < slots:
                mine = dquery[pl.ds(t * points, points), :]
                own_grad[t] = acc + dot(mine, w_query[...], NT)
            else:
                far_grad[t - slots] = acc.astype(BF16)

    for pair in range(4):
        for s in range(slots):
            heads(s, pair)
    returns = []
    for i in range(4):
        part = pl.ds(i % 2 * 64, 64)
        returns.append(
            (
                [far_grad.at[2 * d + i // 2, part] for d in range(4)],
                [back.at[d, i // 2, part] for d in range(4)],
                *behind[i],
            )
        )
    chain = sums()
    for at in range(1, 7):
        next(chain)
        if at == 1:
            terms()
        for i in range(4):
            if at == RETURN_AT[i]:
                exchange_start(here, *returns[i])
            if at == RETURN_AT[i] + 1:
                exchange_relay(here, *returns[i])
    for i in range(4):
        exchange_finish(here, *returns[i])
    acc = own_grad[...]
    for d in range(4):
        acc = acc + back[d].astype(F32)
    feat_grad[...] = acc.astype(BF16)
    next(chain)


def layer(patch_count, point_count, neighbours, neighbour_points, feats, w_query, w_key, w_value, out_grad):
    slots, points, width = feats.shape
    entries = slots * (neighbours.shape[-1] + 1)
    own, every = slots * points, entries * points
    dma = pltpu.SemaphoreType.DMA
    smem = pl.BlockSpec(memory_space=pltpu.SMEM)
    vmem = pl.BlockSpec(memory_space=pltpu.VMEM)
    hbm = pl.BlockSpec(memory_space=pl.ANY)

    def held(*shape, kind=BF16):
        return pltpu.VMEM(shape, kind)

    return pl.pallas_call(
        layer_kernel,
        out_shape=[
            jax.ShapeDtypeStruct((slots, points, width), BF16),
            jax.ShapeDtypeStruct((slots, points, width), BF16),
            jax.ShapeDtypeStruct((3, 512, 512), BF16),
        ],
        in_specs=[smem] * 4 + [vmem] + [hbm] * 4,
        out_specs=[vmem] * 3,
        scratch_shapes=[
            held(width, width), held(width, width), held(width, width), held(slots, points, width),
            held(5 * slots, points, width),
            held(every, width),
            held(width, every),
            held(every, width), held(every, width),
            held(own, width), held(own, width),
            held(every, width), held(every, width),
            held(entries, points, width, kind=F32),
            held(slots, points, width, kind=F32),
            held(4 * slots, points, width),
            held(4, slots, points, width),
            held(3, 256, 512), held(3, 256, 512, kind=F32),
            held(3, 256, 512), held(3, 256, 512),
            held(3, 3, 64, 512), held(3, 4, 64, 128),
            held(3, 15, 16, 128), held(4, 3, 16, 128),
            dma((5,)),
            dma((3, 4)), dma((3, 4)),
            dma((3, 3)), dma((3, 3)),
            dma((3,)), dma((3,)),
            dma((3,)), dma((3,)),
            dma((3,)), dma((3,)),
            dma((3, 3)), dma((3, 3)),
            dma((3, 4)), dma((3, 4)),
            *exchange_scratch(64),
            *exchange_scratch(16),
            *exchange_scratch(16),
            *exchange_scratch(16),
            *exchange_scratch(16),
        ],
        compiler_params=pltpu.CompilerParams(
            collective_id=0, has_side_effects=True, vmem_limit_bytes=VMEM_LIMIT
        ),
        name="layer",
    )(patch_count, point_count, neighbours, neighbour_points, feats, w_query, w_key, w_value, out_grad)


def finish_kernel(mixed, feat_grad, summed, *rest):
    outs, (rows, sums, arrive, leave) = rest[:5], rest[5:]
    groups = [[(summed.at[(i + 1) % 3], sums.at[i])] for i in range(3)]
    groups += [[(mixed, rows.at[0])], [(feat_grad, rows.at[1])]]
    held = [sums.at[0], sums.at[1], sums.at[2], rows.at[0], rows.at[1]]
    outs = [*outs[2:], *outs[:2]]
    loads, n = [], 0
    for group in groups:
        loads.append([])
        for src, dst in group:
            loads[-1].append(pltpu.make_async_copy(src, dst, arrive.at[n]))
            loads[-1][-1].start()
            n += 1
    stores = []
    for i, group in enumerate(loads):
        for copy in group:
            copy.wait()
        stores.append(pltpu.make_async_copy(held[i], outs[i], leave.at[i]))
        stores[-1].start()
    for copy in stores:
        copy.wait()


def finish(mixed, feat_grad, summed):
    hbm = pl.BlockSpec(memory_space=pl.ANY)
    width = mixed.shape[2]
    return pl.pallas_call(
        finish_kernel,
        out_shape=[jax.ShapeDtypeStruct(mixed.shape, BF16)] * 2
        + [jax.ShapeDtypeStruct((width, width), BF16)] * 3,
        in_specs=[hbm] * 3,
        out_specs=[hbm] * 5,
        scratch_shapes=[
            pltpu.VMEM((2, *mixed.shape), BF16),
            pltpu.VMEM((3, width, width), BF16),
            pltpu.SemaphoreType.DMA((5,)),
            pltpu.SemaphoreType.DMA((5,)),
        ],
        compiler_params=pltpu.CompilerParams(vmem_limit_bytes=VMEM_LIMIT),
        name="finish",
    )(mixed, feat_grad, summed)


def body(
    feats, w_query, w_key, w_value, out_grad, patch_count, point_count, neighbours, neighbour_points
):
    slots, points, width = (feats.shape[2], feats.shape[3], feats.shape[4])
    mixed, feat_grad, summed = layer(
        patch_count, point_count, neighbours, neighbour_points,
        feats.reshape(slots, points, width), w_query, w_key, w_value,
        out_grad.reshape(slots, points, width),
    )
    mixed, feat_grad, *sums = finish(mixed, feat_grad, summed)
    return (mixed.reshape(feats.shape), feat_grad.reshape(feats.shape), *sums)


def solution(mesh):
    return jax.shard_map(
        body,
        mesh=mesh,
        in_specs=(
            P("gx", "gy", None, None, None),
            P(),
            P(),
            P(),
            P("gx", "gy", None, None, None),
            P("gx", "gy"),
            P("gx", "gy", None),
            P("gx", "gy", None, None),
            P("gx", "gy", None, None),
        ),
        out_specs=(P("gx", "gy", None, None, None), P("gx", "gy", None, None, None), P(), P(), P()),
        check_vma=False,
    )
```
